32 devices in a mesh: groups: 2 (over y), dp: 4 (over x, core), ctx: 4 (over z).
Axes of the slice: x: 2, y: 2, z: 4, core: 2. Of those that a mesh axis runs over, the one named last changes fastest.
Arguments:
- normed_input: bfloat16 [8, 1024, 4096], P(('groups', 'dp'), 'ctx'), parts along dimension 0, may hold values from -6 to 6
- query_weight: bfloat16 [4096, 1024], P(('dp', 'ctx')), may hold values from -0.09375 to 0.09375
- key_vectors: bfloat16 [8, 1024, 1024], P(('groups', 'dp'), 'ctx'), parts along dimension 0, may hold values from -6 to 6
- value_vectors: bfloat16 [8, 1024, 1024], P(('groups', 'dp'), 'ctx'), parts along dimension 0, may hold values from -6 to 6
- input_gate: float32 [8, 4, 1024], P(('groups', 'dp'), None, 'ctx'), parts along dimension 0, may hold values from -16 to 210
- forget_gate: float32 [8, 4, 1024], P(('groups', 'dp'), None, 'ctx'), parts along dimension 0
- resets: int32 [8, 1024], P(('groups', 'dp'), 'ctx'), parts along dimension 0, may hold values 0 or 1
Outputs:
- hidden: bfloat16 [8, 1024, 1024], P(('groups', 'dp'), 'ctx'), parts along dimension 0
The draws below stay inside these ranges and needn't reach their ends.
There are 2 independent parts, one for each index of `groups`. The reference program is written for one: setup_inputs(seed, part) draws one part's arguments, and reference() takes and returns one part's arrays. A program takes and returns all parts, laid end to end along the dimension named above; an argument that names none is the same for every part. Nothing has to cross between parts.
Inputs may be any that keep to these rules, and one draw needn't show every extreme that they name: `resets`: 1 where a new document begins at that position.
All inputs are finite; a program needn't handle non-finite values. No bound on the sum of `resets` on one device may be relied on, other than what follows from the above.
Results may differ from the reference program's by a relative error of at most 0.009.
Values may be sent and summed in bfloat16 or wider, within the bound.
A program may use at most 128 MiB of HBM per device.

```python
import math
import jax
import jax.numpy as jnp
from jax import lax

D = 4096
LOCAL_HEADS = 4
DQK = 256
DV = 256
TOK_DEV = 256
SEQUENCE_LENGTH = 1024
GROUP_SEQUENCES = 4


def head_ranking(one_key):
    return jax.random.permutation(one_key, LOCAL_HEADS)


def draw_forget_gate(key, part):
    random_subkeys = jax.random.split(jax.random.fold_in(key, 11), 7)
    ranking = jax.vmap(head_ranking)(jax.random.split(random_subkeys[0], GROUP_SEQUENCES))
    slow_head = ranking < LOCAL_HEADS // 2
    head_shape = (GROUP_SEQUENCES, LOCAL_HEADS, 1, 1)
    slow_rate = jnp.exp(jax.random.uniform(random_subkeys[1], head_shape, minval=math.log(0.2), maxval=math.log(0.8))) / SEQUENCE_LENGTH
    fast_rate = jnp.exp(jax.random.uniform(random_subkeys[2], head_shape, minval=math.log(1.0 / 50.0), maxval=math.log(1.0 / 30.0)))
    base_rate = jnp.where(slow_head[:, :, None, None], slow_rate, fast_rate)
    block_count = SEQUENCE_LENGTH // TOK_DEV
    device_factor = jnp.exp(jax.random.uniform(random_subkeys[3], (GROUP_SEQUENCES, LOCAL_HEADS, block_count, 1), minval=math.log(0.5), maxval=math.log(2.0)))
    token_factor = jnp.exp(jax.random.uniform(random_subkeys[4], (GROUP_SEQUENCES, LOCAL_HEADS, block_count, TOK_DEV), minval=math.log(0.5), maxval=math.log(2.0)))
    decay_rate = (base_rate * device_factor * token_factor).reshape(GROUP_SEQUENCES, LOCAL_HEADS, SEQUENCE_LENGTH)
    stable_mask = -decay_rate - jnp.log(-jnp.expm1(-decay_rate))
    sudden_mask = jax.random.bernoulli(random_subkeys[5], 2.0 / SEQUENCE_LENGTH, (GROUP_SEQUENCES, 1, SEQUENCE_LENGTH))
    sudden_keep = jax.random.uniform(random_subkeys[6], (GROUP_SEQUENCES, LOCAL_HEADS, SEQUENCE_LENGTH), minval=0.5, maxval=0.8)
    return jnp.where(sudden_mask, jnp.log(sudden_keep / (1.0 - sudden_keep)), stable_mask)


def draw_input_gate(key, part):
    random_subkeys = jax.random.split(jax.random.fold_in(key, 23), 1)
    gate_shape = (GROUP_SEQUENCES, LOCAL_HEADS, SEQUENCE_LENGTH)
    return jnp.clip(-8.0 + 2.5 * jax.random.normal(random_subkeys[0], gate_shape), -16.0, 0.0)


def touch_ends(values, own_key, smallest, top_value):
    extent = values.shape
    index_at = [jax.random.randint(jax.random.fold_in(own_key, axis), (), 0, extent[axis]) for axis in range(len(extent))]
    values = values.at[tuple(index_at)].set(smallest)
    longest = extent.index(max(extent))
    index_at[longest] = (index_at[longest] + 1) % extent[longest]
    return values.at[tuple(index_at)].set(top_value)


def steps_of(rng, dims, shards, least, high):
    def one(axis_at, parts):
        draws = jax.random.uniform(jax.random.fold_in(jax.random.fold_in(rng, 6), axis_at), (parts,), jnp.float32, least / len(shards), high / len(shards))
        return jnp.repeat(jnp.exp(draws), dims[axis_at] // parts).reshape((-1,) + (1,) * (len(dims) - axis_at - 1))

    level = one(*shards[0])
    for cut in shards[1:]:
        level = level * one(*cut)
    return level


def centred(own_key, shape, deviation, reach, cuts=(), kind=jnp.bfloat16):
    result = jax.random.normal(own_key, shape, jnp.float32) * deviation
    if len(cuts) > 0:
        result = steps_of(own_key, shape, cuts, -0.22, 0.18) * result
    return jnp.clip(result, min=-reach, max=reach).astype(kind)


def setup_inputs(seed: int = 0, part: int = 0) -> dict:
    keys = jax.random.split(jax.random.key(seed), 8)
    part_splits = jax.random.split(jax.random.fold_in(keys[7], part), 8)
    return {
        "normed_input": centred(part_splits[0], (GROUP_SEQUENCES, SEQUENCE_LENGTH, D), 1.0, 6.0, ((0, 4), (1, 4))),
        "query_weight": centred(keys[1], (D, LOCAL_HEADS * DQK), D ** -0.5, 0.09375, ((0, 16),)),
        "key_vectors": centred(part_splits[2], (GROUP_SEQUENCES, SEQUENCE_LENGTH, LOCAL_HEADS * DQK), 1.0, 6.0, ((0, 4), (1, 4))),
        "value_vectors": centred(part_splits[3], (GROUP_SEQUENCES, SEQUENCE_LENGTH, LOCAL_HEADS * DV), 1.0, 6.0, ((0, 4), (1, 4))),
        "input_gate": draw_input_gate(jax.random.fold_in(jax.random.fold_in(keys[7], part), 71), part),
        "forget_gate": draw_forget_gate(jax.random.fold_in(jax.random.fold_in(keys[7], part), 71), part),
        "resets": touch_ends((jax.random.randint(part_splits[6], (GROUP_SEQUENCES, SEQUENCE_LENGTH), 0, SEQUENCE_LENGTH) < 1).astype(jnp.int32), jax.random.fold_in(part_splits[6], 1), 0, 1),
    }


very_low = -1.0e30


def wide_einsum(form, left, right):
    return jnp.einsum(form, left.astype(jnp.float32), right.astype(jnp.float32), precision=lax.Precision.HIGHEST)


def block_step(state, block):
    matrix_memory, normer, log_max = state
    query_tile, key_block, value_tile, gate_block, forget_block, flag_block = block
    score_factor = DQK ** -0.5
    reset_count = jnp.cumsum(flag_block)
    cumulative = jnp.cumsum(forget_block, axis=1)
    positions = jnp.arange(flag_block.shape[0])
    linked = jnp.logical_and(reset_count[:, None] == reset_count[None, :], positions[:, None] >= positions[None, :])
    exponent = jnp.where(linked[None], cumulative[:, :, None] - cumulative[:, None, :] + gate_block[:, None, :], very_low)
    carried = jnp.where(reset_count[None, :] == 0, cumulative + log_max[:, None], very_low)
    row_max = jnp.maximum(jnp.max(exponent, axis=2), carried)
    scores = wide_einsum("thk,shk->hts", query_tile, key_block) * score_factor
    weighted_scores = (jnp.exp(exponent - row_max[:, :, None]) * scores).astype(jnp.bfloat16)
    carry_scale = jnp.exp(carried - row_max)
    cross_numerator = wide_einsum("ngu,gus->ngs", query_tile, matrix_memory.astype(jnp.bfloat16)) * score_factor
    inter_den = wide_einsum("thk,hk->th", query_tile, normer.astype(jnp.bfloat16)) * score_factor
    numerator = wide_einsum("hts,shv->thv", weighted_scores, value_tile)
    numerator = numerator + carry_scale.T[:, :, None] * cross_numerator
    denominator = jnp.sum(weighted_scores.astype(jnp.float32), axis=2).T + carry_scale.T * inter_den
    floor_value = jnp.exp(jnp.maximum(-row_max, 0.0)).T
    hidden = numerator / jnp.maximum(jnp.abs(denominator), floor_value)[:, :, None]
    chain_total = cumulative[:, -1]
    end_expo = jnp.where((reset_count == reset_count[-1])[None, :], chain_total[:, None] - cumulative + gate_block, very_low)
    keep_expo = jnp.where(reset_count[-1] == 0, chain_total + log_max, very_low)
    new_max = jnp.maximum(jnp.max(end_expo, axis=1), keep_expo)
    token_weight = jnp.exp(end_expo - new_max[:, None])
    retain_weight = jnp.exp(keep_expo - new_max)
    key_weighted = (key_block.astype(jnp.float32) * token_weight.T[:, :, None]).astype(jnp.bfloat16)
    matrix_memory = retain_weight[:, None, None] * matrix_memory + wide_einsum("oga,ogu->gau", key_weighted, value_tile)
    normer = retain_weight[:, None] * normer + jnp.sum(key_weighted.astype(jnp.float32), axis=0)
    return (matrix_memory, normer, new_max), hidden


def reference(normed_input, query_weight, key_vectors, value_vectors, input_gate, forget_gate, resets):
    projected = jnp.dot(normed_input.reshape(GROUP_SEQUENCES * SEQUENCE_LENGTH, D).astype(jnp.float32), query_weight.astype(jnp.float32), precision=lax.Precision.HIGHEST).astype(jnp.bfloat16)
    projected = projected.reshape(GROUP_SEQUENCES, SEQUENCE_LENGTH, LOCAL_HEADS, DQK)
    key_heads = key_vectors.reshape(GROUP_SEQUENCES, SEQUENCE_LENGTH, LOCAL_HEADS, DQK)
    value_heads = value_vectors.reshape(GROUP_SEQUENCES, SEQUENCE_LENGTH, LOCAL_HEADS, DV)
    log_forget = jax.nn.log_sigmoid(forget_gate)
    block_len = TOK_DEV
    block_count = SEQUENCE_LENGTH // block_len

    def one_sequence(sequence_item):
        query_seq, key_seq, value_seq, gate_seq, forget_seq, flag_seq = sequence_item
        blocks = (
            query_seq.reshape(block_count, block_len, LOCAL_HEADS, DQK),
            key_seq.reshape(block_count, block_len, LOCAL_HEADS, DQK),
            value_seq.reshape(block_count, block_len, LOCAL_HEADS, DV),
            gate_seq.reshape(LOCAL_HEADS, block_count, block_len).transpose(1, 0, 2),
            forget_seq.reshape(LOCAL_HEADS, block_count, block_len).transpose(1, 0, 2),
            flag_seq.reshape(block_count, block_len),
        )
        start_state = (
            jnp.zeros((LOCAL_HEADS, DQK, DV), jnp.float32),
            jnp.zeros((LOCAL_HEADS, DQK), jnp.float32),
            jnp.full((LOCAL_HEADS,), very_low, jnp.float32),
        )
        final_state, hidden = lax.scan(block_step, start_state, blocks)
        return hidden.reshape(SEQUENCE_LENGTH, LOCAL_HEADS * DV)

    hidden = lax.map(one_sequence, (projected, key_heads, value_heads, input_gate, log_forget, resets))
    return hidden.astype(jnp.bfloat16)
```

```python
import functools

import jax
import jax.numpy as jnp
from jax import lax
from jax.experimental import pallas as pl
from jax.experimental.pallas import tpu as pltpu
from jax.sharding import PartitionSpec as P

very_low = -1e30
shared_columns = 384
MESH = pl.DeviceIdType.MESH


def dot(a, b, dims=((1,), (0,))):
    return lax.dot_general(a, b, (dims, ((), ())), preferred_element_type=jnp.float32)


def kernel(
    spread, Z, heads, x_hbm, w_hbm, k_hbm, v_hbm, ig_ref, fg_ref, rs_ref, out_ref,
    xv, kv, vv, wown, wbuf, acc, prob, stack, imax_scr, own_mem, own_info,
    mem_in, info_in, mem_out, info_out,
    lsem, zsend, zrecv, xsend, xrecv, ysend, yrecv, csend, crecv, ssend, srecv,
):
    y = lax.axis_index("groups")
    d = lax.axis_index("dp")
    z = lax.axis_index("ctx")
    x, c = d // 2, d % 2
    up, down = (y, d, z + 1), (y, d, z - 1)
    across = (y, (1 - x) * 2 + c, z)
    over = (1 - y, d, z)
    mate = (y, x * 2 + 1 - c, z)
    length, features = xv.shape
    dk = kv.shape[1] // heads
    dv = vv.shape[1] // heads
    factor = dk ** (-0.5)
    width = acc.shape[1]
    rows = wbuf.shape[1]
    A = shared_columns

    local = [
        pltpu.make_async_copy(k_hbm.at[0], kv, lsem.at[0]),
        pltpu.make_async_copy(v_hbm.at[0], vv, lsem.at[1]),
        pltpu.make_async_copy(x_hbm.at[0], xv, lsem.at[2]),
        pltpu.make_async_copy(w_hbm, wown, lsem.at[3]),
    ]
    for one in local:
        one.start()

    barrier = pltpu.get_barrier_semaphore()

    def greet(device):
        pl.semaphore_signal(barrier, inc=1, device_id=device, device_id_type=MESH)

    @pl.when(z < Z - 1)
    def _():
        greet(up)

    @pl.when(z > 0)
    def _():
        greet(down)

    base = 0
    if spread:
        for device in (across, over, mate):
            greet(device)
        base = 3
    pl.semaphore_wait(
        barrier, base + jnp.where(z > 0, 1, 0) + jnp.where(z < Z - 1, 1, 0)
    )

    def columns(part):
        if part == 0:
            return pl.ds(pl.multiple_of(y * A, 128), A)
        if part == 1:
            return pl.ds(pl.multiple_of((1 - y) * A, 128), A)
        return pl.ds(2 * A, width - 2 * A)

    def shard(xx, cc, zz):
        return (xx * 2 + cc) * Z + zz

    def remote(xx, cc, zz, part, send, recv, device, own=False):
        there = wbuf.at[shard(xx, cc, zz), :, columns(part)]
        here = w_hbm.at[:, columns(part)] if own else there
        return pltpu.make_async_remote_copy(
            src_ref=here, dst_ref=there, send_sem=send, recv_sem=recv,
            device_id=device, device_id_type=MESH,
        )

    def z_copy(way, zz, part, own=False):
        device = up if way == 0 else down
        return remote(x, c, zz, part, zsend.at[way, zz, part // 2], zrecv.at[zz, part // 2], device, own)

    def x_copy(xx, zz, part, own=False):
        return remote(xx, c, zz, part, xsend.at[zz, part // 2], xrecv.at[zz, part // 2], across, own)

    def y_copy(xx, zz, part):
        return remote(xx, c, zz, part, ysend.at[xx, zz], yrecv.at[xx, zz], over)

    def c_copy(xx, cc, zz, part, own=False):
        return remote(xx, cc, zz, part, csend.at[xx, zz, part], crecv.at[xx, zz, part], mate, own)

    if spread:
        for part in (0, 2):
            @pl.when(z < Z - 1)
            def _():
                z_copy(0, z, part, True).start()

            @pl.when(z > 0)
            def _():
                z_copy(1, z, part, True).start()

            x_copy(x, z, part, True).start()
        for part in (0, 1, 2):
            c_copy(x, c, z, part, True).start()

    g = ig_ref[0]
    f = fg_ref[0]
    stack[...] = jnp.zeros_like(stack)
    stack[0:heads, :] = jnp.minimum(f, 0.0) - jnp.log1p(jnp.exp(-jnp.abs(f)))
    stack[4:5, :] = rs_ref[...].astype(jnp.float32)
    run = stack[0:8, :]
    lane = lax.broadcasted_iota(jnp.int32, run.shape, 1)
    hop = 1
    while hop < length:
        run = run + jnp.where(lane >= hop, pltpu.roll(run, hop, 1), 0.0)
        hop *= 2
    stack[0:8, :] = run
    stack[8:8 + heads, :] = g
    cols = stack[...].T
    count_row, count_col = run[4:5, :], cols[:, 4:5]
    count_last = run[4:5, length - 1:length]

    def cum_col(h):
        return cols[:, h:h + 1]

    def cum_last(h):
        return run[h:h + 1, length - 1:length]

    for one in local[:2]:
        one.wait()

    for h in range(heads):
        end_row = jnp.where(count_row == count_last, cum_last(h) - run[h:h + 1, :] + g[h:h + 1, :], very_low)
        top = jnp.max(end_row, axis=1, keepdims=True)
        end_col = jnp.where(
            count_col == count_last, cum_last(h) - cum_col(h) + cols[:, 8 + h:9 + h], very_low
        )
        weighted = (
            kv[:, h * dk:(h + 1) * dk].astype(jnp.float32) * jnp.exp(end_col - top)
        ).astype(jnp.bfloat16)
        own_mem[h] = dot(weighted, vv[:, h * dv:(h + 1) * dv], ((0,), (0,)))
        own_info[h:h + 1, :] = jnp.sum(weighted.astype(jnp.float32), axis=0, keepdims=True)
        own_info[heads + h:heads + h + 1, :] = jnp.broadcast_to(top, (1, dk))

    def info_copy():
        return pltpu.make_async_remote_copy(
            src_ref=info_out, dst_ref=info_in, send_sem=ssend.at[heads], recv_sem=srecv.at[heads],
            device_id=up, device_id_type=MESH,
        )

    def mem_copy(h):
        return pltpu.make_async_remote_copy(
            src_ref=mem_out.at[h], dst_ref=mem_in.at[h], send_sem=ssend.at[h], recv_sem=srecv.at[h],
            device_id=up, device_id_type=MESH,
        )

    def pass_state():
        @pl.when(z > 0)
        def _():
            info_copy().wait_recv()

        @pl.when(z == 0)
        def _():
            mem_in[...] = jnp.zeros_like(mem_in)
            info_in[0:heads, :] = jnp.zeros((heads, dk), jnp.float32)
            info_in[heads:, :] = jnp.full((heads, dk), very_low, jnp.float32)

        @pl.when(z < Z - 1)
        def _():
            info = info_in[...]
            own = own_info[...]
            early, late = [], []
            for h in range(heads):
                gap = jnp.where(count_last > 0, very_low, cum_last(h))
                shifted = info[heads + h:heads + h + 1, :] + gap
                top = own[heads + h:heads + h + 1, :]
                both = jnp.maximum(shifted, top)
                early.append(jnp.exp(shifted - both))
                late.append(jnp.exp(top - both))
                info_out[h:h + 1, :] = early[h] * info[h:h + 1, :] + late[h] * own[h:h + 1, :]
                info_out[heads + h:heads + h + 1, :] = both
            info_copy().start()
            for h in range(heads):
                @pl.when(z > 0)
                def _():
                    mem_copy(h).wait_recv()

                mem_out[h] = (
                    early[h][:, 0:1] * mem_in[h].astype(jnp.float32) + late[h][:, 0:1] * own_mem[h]
                ).astype(jnp.bfloat16)
                mem_copy(h).start()

        @pl.when(z == Z - 1)
        def _():
            @pl.when(z > 0)
            def _():
                for h in range(heads):
                    mem_copy(h).wait_recv()

    if spread:
        @pl.when(z == 0)
        def _():
            pass_state()
    else:
        pass_state()

    row_at = lax.broadcasted_iota(jnp.int32, (length, length), 0)
    col_at = lax.broadcasted_iota(jnp.int32, (length, length), 1)
    linked = jnp.logical_and(count_col == count_row, row_at >= col_at)
    for h in range(heads):
        exponent = jnp.where(linked, cum_col(h) - run[h:h + 1, :] + g[h:h + 1, :], very_low)
        top = jnp.max(exponent, axis=1, keepdims=True)
        imax_scr[:, h:h + 1] = top
        prob[h] = jnp.exp(exponent - top) * factor

    for one in local[2:]:
        one.wait()

    def multiply(at, piece):
        part = xv[:, pl.ds(pl.multiple_of(at * rows, 128), rows)]
        acc[...] += dot(part, piece)

    if spread:
        acc[...] = dot(xv[:, pl.ds(pl.multiple_of(shard(x, c, z) * rows, 128), rows)], wown[...])

        def places(q, low):
            below, above = z - q, z + q
            yield below, jnp.logical_and(q >= low, jnp.logical_and(q < Z, below >= 0))
            yield above, jnp.logical_and(q >= max(low, 1), above < Z)

        def one_round(r, carry):
            for way, (zz, ok) in enumerate(places(r, 1)):
                @pl.when(ok)
                def _():
                    for part in (0, 2):
                        z_copy(way, zz, part).wait_recv()

                        @pl.when(z < Z - 1 if way == 0 else z > 0)
                        def _():
                            z_copy(way, zz, part).start()

                        x_copy(x, zz, part).start()
                        if part == 0:
                            y_copy(x, zz, 0).start()
                        c_copy(x, c, zz, part).start()

            for zz, ok in places(r - 1, 0):
                @pl.when(ok)
                def _():
                    for part in (0, 2):
                        x_copy(1 - x, zz, part).wait_recv()
                        if part == 0:
                            y_copy(1 - x, zz, 0).start()
                        c_copy(1 - x, c, zz, part).start()

            @pl.when(z == r)
            def _():
                pass_state()

            for zz, ok in places(r - 1, 1):
                @pl.when(ok)
                def _():
                    y_copy(x, zz, 1).wait_recv()
                    c_copy(x, c, zz, 1).start()
                    multiply(shard(x, c, zz), wbuf[shard(x, c, zz)])

            for zz, ok in places(r - 2, 0):
                @pl.when(ok)
                def _():
                    y_copy(1 - x, zz, 1).wait_recv()
                    c_copy(1 - x, c, zz, 1).start()
                    multiply(shard(1 - x, c, zz), wbuf[shard(1 - x, c, zz)])

                @pl.when(ok)
                def _():
                    for part in (0, 1, 2):
                        c_copy(x, 1 - c, zz, part).wait_recv()
                    multiply(shard(x, 1 - c, zz), wbuf[shard(x, 1 - c, zz)])

            for zz, ok in places(r - 3, 0):
                @pl.when(ok)
                def _():
                    for part in (0, 1, 2):
                        c_copy(1 - x, 1 - c, zz, part).wait_recv()
                    multiply(shard(1 - x, 1 - c, zz), wbuf[shard(1 - x, 1 - c, zz)])

            return carry

        lax.fori_loop(1, Z + 3, one_round, 0)
    else:
        acc[...] = jnp.zeros_like(acc)

        def one_block(at, carry):
            multiply(at, wown[pl.ds(pl.multiple_of(at * rows, 16), rows), :])
            return carry

        lax.fori_loop(0, features // rows, one_block, 0)

    info = info_in[...]
    for h in range(heads):
        q = acc[:, h * dk:(h + 1) * dk].astype(jnp.bfloat16)
        values = vv[:, h * dv:(h + 1) * dv]
        scores = dot(q, kv[:, h * dk:(h + 1) * dk], ((1,), (1,)))
        weighted = (scores * prob[h]).astype(jnp.bfloat16)
        inner = dot(weighted, values)
        inner_den = jnp.sum(weighted.astype(jnp.float32), axis=1, keepdims=True)
        cross = dot(q, mem_in[h])
        normer = info[h:h + 1, :].astype(jnp.bfloat16).astype(jnp.float32)
        cross_den = jnp.sum(q.astype(jnp.float32) * normer, axis=1, keepdims=True)
        top = imax_scr[:, h:h + 1]
        carried = jnp.where(count_col == 0, cum_col(h) + info[heads + h:heads + h + 1, 0:1], very_low)
        row_max = jnp.maximum(top, carried)
        a = jnp.exp(top - row_max)
        b = jnp.exp(carried - row_max) * factor
        den = a * inner_den + b * cross_den
        inverse = 1.0 / jnp.maximum(jnp.abs(den), jnp.exp(jnp.maximum(-row_max, 0.0)))
        hidden = (a * inverse) * inner + (b * inverse) * cross
        out_ref[0, :, h * dv:(h + 1) * dv] = hidden.astype(jnp.bfloat16)

    @pl.when(z < Z - 1)
    def _():
        info_copy().wait_send()
        for h in range(heads):
            mem_copy(h).wait_send()

    if spread:
        def drain(zz, carry):
            for part in (0, 2):
                @pl.when(jnp.logical_and(z < Z - 1, zz <= z))
                def _():
                    z_copy(0, zz, part).wait_send()

                @pl.when(jnp.logical_and(z > 0, zz >= z))
                def _():
                    z_copy(1, zz, part).wait_send()

                x_copy(x, zz, part).wait_send()

            @pl.when(zz != z)
            def _():
                y_copy(x, zz, 0).wait_send()

            y_copy(1 - x, zz, 0).wait_send()
            for xx in (x, 1 - x):
                for part in (0, 1, 2):
                    c_copy(xx, c, zz, part).wait_send()
            return carry

        lax.fori_loop(0, Z, drain, 0)


def body(Z, dp, planes, normed_input, query_weight, key_vectors, value_vectors, input_gate, forget_gate, resets):
    _, length, features = normed_input.shape
    heads = input_gate.shape[1]
    width = query_weight.shape[1]
    dk = key_vectors.shape[2] // heads
    dv = value_vectors.shape[2] // heads
    spread = dp == 4 and planes == 2 and query_weight.shape[0] % 128 == 0
    if spread:
        rows = query_weight.shape[0]
        weight = query_weight
    else:
        rows = 256
        weight = lax.all_gather(query_weight, ("dp", "ctx"), axis=0, tiled=True)
    count = features // rows if spread else 1
    dma = pltpu.SemaphoreType.DMA
    any_spec = pl.BlockSpec(memory_space=pl.ANY)
    vmem = pl.BlockSpec(memory_space=pltpu.VMEM)
    return pl.pallas_call(
        functools.partial(kernel, spread, Z, heads),
        out_shape=jax.ShapeDtypeStruct((1, length, heads * dv), jnp.bfloat16),
        in_specs=[any_spec] * 4 + [vmem] * 3,
        out_specs=vmem,
        scratch_shapes=[
            pltpu.VMEM((length, features), jnp.bfloat16),
            pltpu.VMEM((length, heads * dk), jnp.bfloat16),
            pltpu.VMEM((length, heads * dv), jnp.bfloat16),
            pltpu.VMEM(weight.shape, jnp.bfloat16),
            pltpu.VMEM((count, rows, width), jnp.bfloat16),
            pltpu.VMEM((length, width), jnp.float32),
            pltpu.VMEM((heads, length, length), jnp.float32),
            pltpu.VMEM((128, length), jnp.float32),
            pltpu.VMEM((length, 128), jnp.float32),
            pltpu.VMEM((heads, dk, dv), jnp.float32),
            pltpu.VMEM((2 * heads, dk), jnp.float32),
            pltpu.VMEM((heads, dk, dv), jnp.bfloat16),
            pltpu.VMEM((2 * heads, dk), jnp.float32),
            pltpu.VMEM((heads, dk, dv), jnp.bfloat16),
            pltpu.VMEM((2 * heads, dk), jnp.float32),
            dma((4,)),
            dma((2, Z, 2)), dma((Z, 2)),
            dma((Z, 2)), dma((Z, 2)),
            dma((2, Z)), dma((2, Z)),
            dma((2, Z, 3)), dma((2, Z, 3)),
            dma((heads + 1,)), dma((heads + 1,)),
        ],
        compiler_params=pltpu.CompilerParams(
            collective_id=0, has_side_effects=True, vmem_limit_bytes=40 * 1024 * 1024
        ),
        cost_estimate=pl.CostEstimate(
            flops=2 * length * features * width, bytes_accessed=6 * 1024 * 1024, transcendentals=0
        ),
    )(normed_input, weight, key_vectors, value_vectors, input_gate, forget_gate, resets)


def solution(mesh):
    sizes = mesh.shape
    return jax.shard_map(
        functools.partial(body, sizes["ctx"], sizes["dp"], sizes["groups"]),
        mesh=mesh,
        in_specs=(
            P(("groups", "dp"), "ctx", None),
            P(("dp", "ctx"), None),
            P(("groups", "dp"), "ctx", None),
            P(("groups", "dp"), "ctx", None),
            P(("groups", "dp"), None, "ctx"),
            P(("groups", "dp"), None, "ctx"),
            P(("groups", "dp"), "ctx"),
        ),
        out_specs=P(("groups", "dp"), "ctx", None),
        check_vma=False,
    )
```

```python
import functools

import jax
import jax.numpy as jnp
from jax import lax
from jax.experimental import pallas as pl
from jax.experimental.pallas import tpu as pltpu
from jax.sharding import PartitionSpec as P

very_low = -1e30
shared_columns = 384
pieces = 2
MESH = pl.DeviceIdType.MESH


def dot(a, b, dims=((1,), (0,))):
    return lax.dot_general(a, b, (dims, ((), ())), preferred_element_type=jnp.float32)


def kernel(
    spread, Z, heads, x_hbm, w_hbm, k_hbm, v_hbm, ig_hbm, fg_hbm, rs_hbm, out_ref,
    gates, flags, xv, kv, vv, wown, wbuf, acc, prob, stack, imax_scr, own_mem, own_info,
    mem_in, info_in, mem_out, info_out,
    lsem, zsend, zrecv, xsend, xrecv, ysend, yrecv, csend, crecv, ssend, srecv,
):
    y = lax.axis_index("groups")
    d = lax.axis_index("dp")
    z = lax.axis_index("ctx")
    x, c = d // 2, d % 2
    up, down = (y, d, z + 1), (y, d, z - 1)
    across = (y, (1 - x) * 2 + c, z)
    over = (1 - y, d, z)
    mate = (y, x * 2 + 1 - c, z)
    length, features = xv.shape
    dk = kv.shape[1] // heads
    dv = vv.shape[1] // heads
    factor = dk ** (-0.5)
    width = acc.shape[1]
    rows = wbuf.shape[1]
    A = shared_columns

    local = [
        pltpu.make_async_copy(ig_hbm.at[0], gates.at[0, 0:heads], lsem.at[4]),
        pltpu.make_async_copy(fg_hbm.at[0], gates.at[1, 0:heads], lsem.at[5]),
        pltpu.make_async_copy(rs_hbm, flags, lsem.at[6]),
        pltpu.make_async_copy(k_hbm.at[0], kv, lsem.at[0]),
        pltpu.make_async_copy(v_hbm.at[0], vv, lsem.at[1]),
        pltpu.make_async_copy(x_hbm.at[0], xv, lsem.at[2]),
        pltpu.make_async_copy(w_hbm, wown, lsem.at[3]),
    ]
    for one in local:
        one.start()

    barrier = pltpu.get_barrier_semaphore()

    def greet(device):
        pl.semaphore_signal(barrier, inc=1, device_id=device, device_id_type=MESH)

    @pl.when(z < Z - 1)
    def _():
        greet(up)

    @pl.when(z > 0)
    def _():
        greet(down)

    base = 0
    if spread:
        for device in (across, over, mate):
            greet(device)
        base = 3
    pl.semaphore_wait(
        barrier, base + jnp.where(z > 0, 1, 0) + jnp.where(z < Z - 1, 1, 0)
    )

    B = width - 2 * A

    def columns(part):
        if part == 0:
            return pl.ds(pl.multiple_of(y * A, 128), A + B)
        if part == 1:
            return pl.ds(pl.multiple_of(y * (A + B), 128), A)
        return pl.ds(pl.multiple_of((1 - y) * (A + B), 128), A)

    high = rows // pieces

    def shard(xx, cc, zz):
        return (xx * 2 + cc) * Z + zz

    def remote(xx, cc, zz, p, part, send, recv, device, own=False):
        at = pl.ds(p * high if isinstance(p, int) else pl.multiple_of(p * high, 16), high)
        there = wbuf.at[shard(xx, cc, zz), at, columns(part)]
        here = w_hbm.at[at, columns(part)] if own else there
        return pltpu.make_async_remote_copy(
            src_ref=here, dst_ref=there, send_sem=send, recv_sem=recv,
            device_id=device, device_id_type=MESH,
        )

    def z_copy(way, zz, p, own=False):
        device = up if way == 0 else down
        return remote(x, c, zz, p, 0, zsend.at[way, zz, p], zrecv.at[zz, p], device, own)

    def x_copy(xx, zz, p, own=False):
        return remote(xx, c, zz, p, 0, xsend.at[zz, p], xrecv.at[zz, p], across, own)

    def y_copy(xx, zz, p, part):
        return remote(xx, c, zz, p, part, ysend.at[xx, zz, p], yrecv.at[xx, zz, p], over)

    def c_copy(xx, cc, zz, p, part, own=False):
        return remote(
            xx, cc, zz, p, part, csend.at[xx, zz, p, part // 2], crecv.at[xx, zz, p, part // 2], mate, own
        )

    if spread:
        for p in range(pieces):
            @pl.when(z < Z - 1)
            def _():
                z_copy(0, z, p, True).start()

            @pl.when(z > 0)
            def _():
                z_copy(1, z, p, True).start()

            x_copy(x, z, p, True).start()
        for p in range(pieces):
            for part in (0, 2):
                c_copy(x, c, z, p, part, True).start()

    for one in local[:3]:
        one.wait()

    g = gates[0, 0:heads, :]
    f = gates[1, 0:heads, :]
    stack[...] = jnp.zeros_like(stack)
    stack[0:heads, :] = jnp.minimum(f, 0.0) - jnp.log1p(jnp.exp(-jnp.abs(f)))
    stack[4:5, :] = flags[...].astype(jnp.float32)
    run = stack[0:8, :]
    lane = lax.broadcasted_iota(jnp.int32, run.shape, 1)
    hop = 1
    while hop < length:
        run = run + jnp.where(lane >= hop, pltpu.roll(run, hop, 1), 0.0)
        hop *= 2
    stack[0:8, :] = run
    stack[8:8 + heads, :] = g
    cols = stack[...].T
    count_row, count_col = run[4:5, :], cols[:, 4:5]
    count_last = run[4:5, length - 1:length]

    def cum_col(h):
        return cols[:, h:h + 1]

    def cum_last(h):
        return run[h:h + 1, length - 1:length]

    for one in local[3:5]:
        one.wait()

    for h in range(heads):
        end_row = jnp.where(count_row == count_last, cum_last(h) - run[h:h + 1, :] + g[h:h + 1, :], very_low)
        top = jnp.max(end_row, axis=1, keepdims=True)
        end_col = jnp.where(
            count_col == count_last, cum_last(h) - cum_col(h) + cols[:, 8 + h:9 + h], very_low
        )
        weighted = (
            kv[:, h * dk:(h + 1) * dk].astype(jnp.float32) * jnp.exp(end_col - top)
        ).astype(jnp.bfloat16)
        own_mem[h] = dot(weighted, vv[:, h * dv:(h + 1) * dv], ((0,), (0,)))
        own_info[h:h + 1, :] = jnp.sum(weighted.astype(jnp.float32), axis=0, keepdims=True)
        own_info[heads + h:heads + h + 1, :] = jnp.broadcast_to(top, (1, dk))

    def info_copy():
        return pltpu.make_async_remote_copy(
            src_ref=info_out, dst_ref=info_in, send_sem=ssend.at[heads], recv_sem=srecv.at[heads],
            device_id=up, device_id_type=MESH,
        )

    def mem_copy(h):
        return pltpu.make_async_remote_copy(
            src_ref=mem_out.at[h], dst_ref=mem_in.at[h], send_sem=ssend.at[h], recv_sem=srecv.at[h],
            device_id=up, device_id_type=MESH,
        )

    def pass_head(h):
        if h == 0:
            @pl.when(z > 0)
            def _():
                info_copy().wait_recv()

        @pl.when(z > 0)
        def _():
            mem_copy(h).wait_recv()

        @pl.when(z < Z - 1)
        def _():
            def blend(at):
                gap = jnp.where(count_last > 0, very_low, cum_last(at))
                shifted = info_in[heads + at:heads + at + 1, :] + gap
                top = own_info[heads + at:heads + at + 1, :]
                both = jnp.maximum(shifted, top)
                return both, jnp.exp(shifted - both), jnp.exp(top - both)

            if h == 0:
                for at in range(heads):
                    both, early, late = blend(at)
                    info_out[at:at + 1, :] = early * info_in[at:at + 1, :] + late * own_info[at:at + 1, :]
                    info_out[heads + at:heads + at + 1, :] = both
                info_copy().start()
            _, early, late = blend(h)
            mem_out[h] = (
                early[:, 0:1] * mem_in[h].astype(jnp.float32) + late[:, 0:1] * own_mem[h]
            ).astype(jnp.bfloat16)
            mem_copy(h).start()

    @pl.when(z == 0)
    def _():
        mem_in[...] = jnp.zeros_like(mem_in)
        info_in[0:heads, :] = jnp.zeros((heads, dk), jnp.float32)
        info_in[heads:, :] = jnp.full((heads, dk), very_low, jnp.float32)
        for h in range(heads):
            pass_head(h)

    if not spread:
        @pl.when(z > 0)
        def _():
            for h in range(heads):
                pass_head(h)

    row_at = lax.broadcasted_iota(jnp.int32, (length, length), 0)
    col_at = lax.broadcasted_iota(jnp.int32, (length, length), 1)
    linked = jnp.logical_and(count_col == count_row, row_at >= col_at)
    for h in range(heads):
        exponent = jnp.where(linked, cum_col(h) - run[h:h + 1, :] + g[h:h + 1, :], very_low)
        top = jnp.max(exponent, axis=1, keepdims=True)
        imax_scr[:, h:h + 1] = top
        prob[h] = jnp.exp(exponent - top) * factor

    for one in local[5:]:
        one.wait()

    def multiply(at, piece):
        part = xv[:, pl.ds(pl.multiple_of(at * rows, 128), rows)]
        acc[...] += dot(part, piece)

    if spread:
        state_steps = [-(-2 * pieces * (h + 1) // 5) for h in range(heads)]
        acc[...] = dot(xv[:, pl.ds(pl.multiple_of(shard(x, c, z) * rows, 128), rows)], wown[...])

        def places(s, low):
            q = (s + pieces) // pieces - 1
            p = (s + pieces) % pieces
            below, above = z - q, z + q
            yield below, p, jnp.logical_and(q >= low, jnp.logical_and(q < Z, below >= 0))
            yield above, p, jnp.logical_and(q >= max(low, 1), above < Z)

        def take(xx, cc, zz, p):
            @pl.when(p == pieces - 1)
            def _():
                multiply(shard(xx, cc, zz), wbuf[shard(xx, cc, zz)])

        def one_step(t, carry):
            for way, (zz, p, ok) in enumerate(places(t, 1)):
                @pl.when(ok)
                def _():
                    z_copy(way, zz, p).wait_recv()

                    @pl.when(z < Z - 1 if way == 0 else z > 0)
                    def _():
                        z_copy(way, zz, p).start()

                    x_copy(x, zz, p).start()
                    y_copy(x, zz, p, 1).start()
                    c_copy(x, c, zz, p, 0).start()

            for zz, p, ok in places(t - 1, 0):
                @pl.when(ok)
                def _():
                    x_copy(1 - x, zz, p).wait_recv()
                    y_copy(1 - x, zz, p, 1).start()
                    c_copy(1 - x, c, zz, p, 0).start()

            for h in range(heads):
                @pl.when(jnp.logical_and(t == z * pieces + state_steps[h], jnp.logical_and(z > 0, z < Z - 1)))
                def _():
                    pass_head(h)

            for zz, p, ok in places(t - 1, 1):
                @pl.when(ok)
                def _():
                    y_copy(x, zz, p, 2).wait_recv()
                    c_copy(x, c, zz, p, 2).start()
                    take(x, c, zz, p)

            for zz, p, ok in places(t - 2, 0):
                @pl.when(ok)
                def _():
                    y_copy(1 - x, zz, p, 2).wait_recv()
                    c_copy(1 - x, c, zz, p, 2).start()
                    take(1 - x, c, zz, p)

                @pl.when(ok)
                def _():
                    for part in (0, 2):
                        c_copy(x, 1 - c, zz, p, part).wait_recv()
                    take(x, 1 - c, zz, p)

            for zz, p, ok in places(t - 3, 0):
                @pl.when(ok)
                def _():
                    for part in (0, 2):
                        c_copy(1 - x, 1 - c, zz, p, part).wait_recv()
                    take(1 - x, 1 - c, zz, p)

            return carry

        lax.fori_loop(1, Z * pieces + 3, one_step, 0)

        @pl.when(z == Z - 1)
        def _():
            for h in range(heads):
                pass_head(h)

    else:
        acc[...] = jnp.zeros_like(acc)

        def one_block(at, carry):
            multiply(at, wown[pl.ds(pl.multiple_of(at * rows, 16), rows), :])
            return carry

        lax.fori_loop(0, features // rows, one_block, 0)

    info = info_in[...]
    for h in range(heads):
        q = acc[:, h * dk:(h + 1) * dk].astype(jnp.bfloat16)
        values = vv[:, h * dv:(h + 1) * dv]
        scores = dot(q, kv[:, h * dk:(h + 1) * dk], ((1,), (1,)))
        weighted = (scores * prob[h]).astype(jnp.bfloat16)
        inner = dot(weighted, values)
        inner_den = jnp.sum(weighted.astype(jnp.float32), axis=1, keepdims=True)
        cross = dot(q, mem_in[h])
        normer = info[h:h + 1, :].astype(jnp.bfloat16).astype(jnp.float32)
        cross_den = jnp.sum(q.astype(jnp.float32) * normer, axis=1, keepdims=True)
        top = imax_scr[:, h:h + 1]
        carried = jnp.where(count_col == 0, cum_col(h) + info[heads + h:heads + h + 1, 0:1], very_low)
        row_max = jnp.maximum(top, carried)
        a = jnp.exp(top - row_max)
        b = jnp.exp(carried - row_max) * factor
        den = a * inner_den + b * cross_den
        inverse = 1.0 / jnp.maximum(jnp.abs(den), jnp.exp(jnp.maximum(-row_max, 0.0)))
        hidden = (a * inverse) * inner + (b * inverse) * cross
        out_ref[0, :, h * dv:(h + 1) * dv] = hidden.astype(jnp.bfloat16)

    @pl.when(z < Z - 1)
    def _():
        info_copy().wait_send()
        for h in range(heads):
            mem_copy(h).wait_send()

    if spread:
        def drain(s, carry):
            zz, p = s // pieces, s % pieces

            @pl.when(jnp.logical_and(z < Z - 1, zz <= z))
            def _():
                z_copy(0, zz, p).wait_send()

            @pl.when(jnp.logical_and(z > 0, zz >= z))
            def _():
                z_copy(1, zz, p).wait_send()

            x_copy(x, zz, p).wait_send()

            @pl.when(zz != z)
            def _():
                y_copy(x, zz, p, 1).wait_send()

            y_copy(1 - x, zz, p, 1).wait_send()
            for xx in (x, 1 - x):
                for part in (0, 2):
                    c_copy(xx, c, zz, p, part).wait_send()
            return carry

        lax.fori_loop(0, Z * pieces, drain, 0)


def body(Z, dp, planes, normed_input, query_weight, key_vectors, value_vectors, input_gate, forget_gate, resets):
    _, length, features = normed_input.shape
    heads = input_gate.shape[1]
    width = query_weight.shape[1]
    dk = key_vectors.shape[2] // heads
    dv = value_vectors.shape[2] // heads
    spread = dp == 4 and planes == 2 and query_weight.shape[0] % 256 == 0
    if spread:
        rows = query_weight.shape[0]
        weight = query_weight
    else:
        rows = 256
        weight = lax.all_gather(query_weight, ("dp", "ctx"), axis=0, tiled=True)
    count = features // rows if spread else 1
    dma = pltpu.SemaphoreType.DMA
    hbm = pl.BlockSpec(memory_space=pltpu.HBM)
    vmem = pl.BlockSpec(memory_space=pltpu.VMEM)
    return pl.pallas_call(
        functools.partial(kernel, spread, Z, heads),
        out_shape=jax.ShapeDtypeStruct((1, length, heads * dv), jnp.bfloat16),
        in_specs=[hbm] * 7,
        out_specs=vmem,
        scratch_shapes=[
            pltpu.VMEM((2, 8, length), jnp.float32),
            pltpu.VMEM((1, length), jnp.int32),
            pltpu.VMEM((length, features), jnp.bfloat16),
            pltpu.VMEM((length, heads * dk), jnp.bfloat16),
            pltpu.VMEM((length, heads * dv), jnp.bfloat16),
            pltpu.VMEM(weight.shape, jnp.bfloat16),
            pltpu.VMEM((count, rows, width), jnp.bfloat16),
            pltpu.VMEM((length, width), jnp.float32),
            pltpu.VMEM((heads, length, length), jnp.float32),
            pltpu.VMEM((128, length), jnp.float32),
            pltpu.VMEM((length, 128), jnp.float32),
            pltpu.VMEM((heads, dk, dv), jnp.float32),
            pltpu.VMEM((2 * heads, dk), jnp.float32),
            pltpu.VMEM((heads, dk, dv), jnp.bfloat16),
            pltpu.VMEM((2 * heads, dk), jnp.float32),
            pltpu.VMEM((heads, dk, dv), jnp.bfloat16),
            pltpu.VMEM((2 * heads, dk), jnp.float32),
            dma((7,)),
            dma((2, Z, pieces)), dma((Z, pieces)),
            dma((Z, pieces)), dma((Z, pieces)),
            dma((2, Z, pieces)), dma((2, Z, pieces)),
            dma((2, Z, pieces, 2)), dma((2, Z, pieces, 2)),
            dma((heads + 1,)), dma((heads + 1,)),
        ],
        compiler_params=pltpu.CompilerParams(
            collective_id=0, has_side_effects=True, vmem_limit_bytes=40 * 1024 * 1024
        ),
        cost_estimate=pl.CostEstimate(
            flops=2 * length * features * width, bytes_accessed=6 * 1024 * 1024, transcendentals=0
        ),
    )(normed_input, weight, key_vectors, value_vectors, input_gate, forget_gate, resets)


def solution(mesh):
    sizes = mesh.shape
    return jax.shard_map(
        functools.partial(body, sizes["ctx"], sizes["dp"], sizes["groups"]),
        mesh=mesh,
        in_specs=(
            P(("groups", "dp"), "ctx", None),
            P(("dp", "ctx"), None),
            P(("groups", "dp"), "ctx", None),
            P(("groups", "dp"), "ctx", None),
            P(("groups", "dp"), None, "ctx"),
            P(("groups", "dp"), None, "ctx"),
            P(("groups", "dp"), "ctx"),
        ),
        out_specs=P(("groups", "dp"), "ctx", None),
        check_vma=False,
    )
```

```python
import functools

import jax
import jax.numpy as jnp
from jax import lax
from jax.experimental import pallas as pl
from jax.experimental.pallas import tpu as pltpu
from jax.sharding import PartitionSpec as P

very_low = -1e30
shared_columns = 384
pieces = 2
MESH = pl.DeviceIdType.MESH


def dot(a, b, dims=((1,), (0,))):
    return lax.dot_general(a, b, (dims, ((), ())), preferred_element_type=jnp.float32)


def kernel(
    spread, Z, heads, x_hbm, w_hbm, k_hbm, v_hbm, ig_hbm, fg_hbm, rs_hbm, out_ref,
    gates, flags, xv, kv, vv, wown, wbuf, acc, prob, stack, cols, imax_scr, own_mem, own_info,
    mem_in, info_in, mem_out, info_out,
    lsem, zsend, zrecv, xsend, xrecv, ysend, yrecv, csend, crecv, ssend, srecv,
):
    y = lax.axis_index("groups")
    d = lax.axis_index("dp")
    z = lax.axis_index("ctx")
    x, c = d // 2, d % 2
    up, down = (y, d, z + 1), (y, d, z - 1)
    across = (y, (1 - x) * 2 + c, z)
    over = (1 - y, d, z)
    mate = (y, x * 2 + 1 - c, z)
    length, features = xv.shape
    dk = kv.shape[1] // heads
    dv = vv.shape[1] // heads
    factor = dk ** (-0.5)
    width = acc.shape[1]
    rows = wbuf.shape[1]
    A = shared_columns

    local = [
        pltpu.make_async_copy(ig_hbm.at[0], gates.at[0, 0:heads], lsem.at[4]),
        pltpu.make_async_copy(fg_hbm.at[0], gates.at[1, 0:heads], lsem.at[5]),
        pltpu.make_async_copy(rs_hbm, flags, lsem.at[6]),
        pltpu.make_async_copy(k_hbm.at[0], kv, lsem.at[0]),
        pltpu.make_async_copy(v_hbm.at[0], vv, lsem.at[1]),
        pltpu.make_async_copy(x_hbm.at[0], xv, lsem.at[2]),
        pltpu.make_async_copy(w_hbm, wown, lsem.at[3]),
    ]
    for one in local:
        one.start()

    barrier = pltpu.get_barrier_semaphore()

    def greet(device):
        pl.semaphore_signal(barrier, inc=1, device_id=device, device_id_type=MESH)

    @pl.when(z < Z - 1)
    def _():
        greet(up)

    @pl.when(z > 0)
    def _():
        greet(down)

    base = 0
    if spread:
        for device in (across, over, mate):
            greet(device)
        base = 3
    pl.semaphore_wait(
        barrier, base + jnp.where(z > 0, 1, 0) + jnp.where(z < Z - 1, 1, 0)
    )

    B = width - 2 * A

    def columns(part):
        if part == 0:
            return pl.ds(pl.multiple_of(y * A, 128), A + B)
        if part == 1:
            return pl.ds(pl.multiple_of(y * (A + B), 128), A)
        return pl.ds(pl.multiple_of((1 - y) * (A + B), 128), A)

    high = rows // pieces

    def shard(xx, cc, zz):
        return (xx * 2 + cc) * Z + zz

    def remote(xx, cc, zz, p, part, send, recv, device, own=False):
        at = pl.ds(p * high if isinstance(p, int) else pl.multiple_of(p * high, 16), high)
        there = wbuf.at[shard(xx, cc, zz), at, columns(part)]
        here = w_hbm.at[at, columns(part)] if own else there
        return pltpu.make_async_remote_copy(
            src_ref=here, dst_ref=there, send_sem=send, recv_sem=recv,
            device_id=device, device_id_type=MESH,
        )

    def z_copy(way, zz, p, own=False):
        device = up if way == 0 else down
        return remote(x, c, zz, p, 0, zsend.at[way, zz, p], zrecv.at[zz, p], device, own)

    def x_copy(xx, zz, p, own=False):
        return remote(xx, c, zz, p, 0, xsend.at[zz, p], xrecv.at[zz, p], across, own)

    def y_copy(xx, zz, p, part):
        return remote(xx, c, zz, p, part, ysend.at[xx, zz, p], yrecv.at[xx, zz, p], over)

    def c_copy(xx, cc, zz, p, part, own=False):
        return remote(
            xx, cc, zz, p, part, csend.at[xx, zz, p, part // 2], crecv.at[xx, zz, p, part // 2], mate, own
        )

    if spread:
        for p in range(pieces):
            @pl.when(z < Z - 1)
            def _():
                z_copy(0, z, p, True).start()

            @pl.when(z > 0)
            def _():
                z_copy(1, z, p, True).start()

            x_copy(x, z, p, True).start()
        for p in range(pieces):
            for part in (0, 2):
                c_copy(x, c, z, p, part, True).start()

    for one in local[:3]:
        one.wait()

    f = gates[1, 0:heads, :]
    stack[...] = jnp.zeros_like(stack)
    stack[0:heads, :] = jnp.minimum(f, 0.0) - jnp.log1p(jnp.exp(-jnp.abs(f)))
    stack[4:5, :] = flags[...].astype(jnp.float32)
    run = stack[0:8, :]
    lane = lax.broadcasted_iota(jnp.int32, run.shape, 1)
    hop = 1
    while hop < length:
        run = run + jnp.where(lane >= hop, pltpu.roll(run, hop, 1), 0.0)
        hop *= 2
    stack[0:8, :] = run
    stack[8:8 + heads, :] = gates[0, 0:heads, :]
    cols[...] = stack[...].T

    def row(at):
        return stack[at:at + 1, :]

    def col(at):
        return cols[:, at:at + 1]

    def last(at):
        return stack[at:at + 1, length - 1:length]

    def own_state(h):
        end_row = jnp.where(row(4) == last(4), last(h) - row(h) + row(8 + h), very_low)
        top = jnp.max(end_row, axis=1, keepdims=True)
        end_col = jnp.where(col(4) == last(4), last(h) - col(h) + col(8 + h), very_low)
        weighted = (
            kv[:, h * dk:(h + 1) * dk].astype(jnp.float32) * jnp.exp(end_col - top)
        ).astype(jnp.bfloat16)
        own_mem[h] = dot(weighted, vv[:, h * dv:(h + 1) * dv], ((0,), (0,)))
        own_info[h:h + 1, :] = jnp.sum(weighted.astype(jnp.float32), axis=0, keepdims=True)
        own_info[heads + h:heads + h + 1, :] = jnp.broadcast_to(top, (1, dk))

    def decay(h):
        row_at = lax.broadcasted_iota(jnp.int32, (length, length), 0)
        col_at = lax.broadcasted_iota(jnp.int32, (length, length), 1)
        linked = jnp.logical_and(col(4) == row(4), row_at >= col_at)
        exponent = jnp.where(linked, col(h) - row(h) + row(8 + h), very_low)
        top = jnp.max(exponent, axis=1, keepdims=True)
        imax_scr[:, h:h + 1] = top
        prob[h] = jnp.exp(exponent - top) * factor

    def info_copy():
        return pltpu.make_async_remote_copy(
            src_ref=info_out, dst_ref=info_in, send_sem=ssend.at[heads], recv_sem=srecv.at[heads],
            device_id=up, device_id_type=MESH,
        )

    def mem_copy(h):
        return pltpu.make_async_remote_copy(
            src_ref=mem_out.at[h], dst_ref=mem_in.at[h], send_sem=ssend.at[h], recv_sem=srecv.at[h],
            device_id=up, device_id_type=MESH,
        )

    def pass_head(h):
        if h == 0:
            @pl.when(z > 0)
            def _():
                info_copy().wait_recv()

        @pl.when(z > 0)
        def _():
            mem_copy(h).wait_recv()

        @pl.when(z < Z - 1)
        def _():
            def blend(at):
                gap = jnp.where(last(4) > 0, very_low, last(at))
                shifted = info_in[heads + at:heads + at + 1, :] + gap
                top = own_info[heads + at:heads + at + 1, :]
                both = jnp.maximum(shifted, top)
                return both, jnp.exp(shifted - both), jnp.exp(top - both)

            if h == 0:
                for at in range(heads):
                    both, early, late = blend(at)
                    info_out[at:at + 1, :] = early * info_in[at:at + 1, :] + late * own_info[at:at + 1, :]
                    info_out[heads + at:heads + at + 1, :] = both
                info_copy().start()
            _, early, late = blend(h)
            mem_out[h] = (
                early[:, 0:1] * mem_in[h].astype(jnp.float32) + late[:, 0:1] * own_mem[h]
            ).astype(jnp.bfloat16)
            mem_copy(h).start()

    def start_state():
        for one in local[3:5]:
            one.wait()
        for h in range(heads):
            own_state(h)

        @pl.when(z == 0)
        def _():
            mem_in[...] = jnp.zeros_like(mem_in)
            info_in[0:heads, :] = jnp.zeros((heads, dk), jnp.float32)
            info_in[heads:, :] = jnp.full((heads, dk), very_low, jnp.float32)
            for h in range(heads):
                pass_head(h)

    if not spread:
        start_state()

        @pl.when(z > 0)
        def _():
            for h in range(heads):
                pass_head(h)

        for h in range(heads):
            decay(h)
        for one in local[5:]:
            one.wait()

    def multiply(at, piece):
        part = xv[:, pl.ds(pl.multiple_of(at * rows, 128), rows)]
        acc[...] += dot(part, piece)

    if spread:
        state_steps = [-(-2 * pieces * (h + 1) // 5) for h in range(heads)]
        def places(s, low):
            q = (s + pieces) // pieces - 1
            p = (s + pieces) % pieces
            below, above = z - q, z + q
            yield below, p, jnp.logical_and(q >= low, jnp.logical_and(q < Z, below >= 0))
            yield above, p, jnp.logical_and(q >= max(low, 1), above < Z)

        def take(xx, cc, zz, p):
            @pl.when(p == pieces - 1)
            def _():
                multiply(shard(xx, cc, zz), wbuf[shard(xx, cc, zz)])

        def one_step(t, carry):
            for way, (zz, p, ok) in enumerate(places(t, 1)):
                @pl.when(ok)
                def _():
                    z_copy(way, zz, p).wait_recv()

                    @pl.when(z < Z - 1 if way == 0 else z > 0)
                    def _():
                        z_copy(way, zz, p).start()

                    x_copy(x, zz, p).start()
                    y_copy(x, zz, p, 1).start()
                    c_copy(x, c, zz, p, 0).start()

            for zz, p, ok in places(t - 1, 0):
                @pl.when(ok)
                def _():
                    x_copy(1 - x, zz, p).wait_recv()
                    y_copy(1 - x, zz, p, 1).start()
                    c_copy(1 - x, c, zz, p, 0).start()

            for h in range(heads):
                @pl.when(jnp.logical_and(t == z * pieces + state_steps[h], jnp.logical_and(z > 0, z < Z - 1)))
                def _():
                    pass_head(h)

            @pl.when(t == 1)
            def _():
                start_state()
                for one in local[5:]:
                    one.wait()
                acc[...] = dot(
                    xv[:, pl.ds(pl.multiple_of(shard(x, c, z) * rows, 128), rows)], wown[...]
                )

            for h in range(heads):
                @pl.when(t == pieces + 1 + h * (pieces // 2))
                def _():
                    decay(h)

            for zz, p, ok in places(t - 1, 1):
                @pl.when(ok)
                def _():
                    y_copy(x, zz, p, 2).wait_recv()
                    c_copy(x, c, zz, p, 2).start()
                    take(x, c, zz, p)

            for zz, p, ok in places(t - 2, 0):
                @pl.when(ok)
                def _():
                    y_copy(1 - x, zz, p, 2).wait_recv()
                    c_copy(1 - x, c, zz, p, 2).start()
                    take(1 - x, c, zz, p)

                @pl.when(ok)
                def _():
                    for part in (0, 2):
                        c_copy(x, 1 - c, zz, p, part).wait_recv()
                    take(x, 1 - c, zz, p)

            for zz, p, ok in places(t - 3, 0):
                @pl.when(ok)
                def _():
                    for part in (0, 2):
                        c_copy(1 - x, 1 - c, zz, p, part).wait_recv()
                    take(1 - x, 1 - c, zz, p)

            return carry

        lax.fori_loop(1, Z * pieces + 3, one_step, 0)

        @pl.when(z == Z - 1)
        def _():
            for h in range(heads):
                pass_head(h)

    else:
        acc[...] = jnp.zeros_like(acc)

        def one_block(at, carry):
            multiply(at, wown[pl.ds(pl.multiple_of(at * rows, 16), rows), :])
            return carry

        lax.fori_loop(0, features // rows, one_block, 0)

    info = info_in[...]
    for h in range(heads):
        q = acc[:, h * dk:(h + 1) * dk].astype(jnp.bfloat16)
        values = vv[:, h * dv:(h + 1) * dv]
        scores = dot(q, kv[:, h * dk:(h + 1) * dk], ((1,), (1,)))
        weighted = (scores * prob[h]).astype(jnp.bfloat16)
        inner = dot(weighted, values)
        inner_den = jnp.sum(weighted.astype(jnp.float32), axis=1, keepdims=True)
        cross = dot(q, mem_in[h])
        normer = info[h:h + 1, :].astype(jnp.bfloat16).astype(jnp.float32)
        cross_den = jnp.sum(q.astype(jnp.float32) * normer, axis=1, keepdims=True)
        top = imax_scr[:, h:h + 1]
        carried = jnp.where(col(4) == 0, col(h) + info[heads + h:heads + h + 1, 0:1], very_low)
        row_max = jnp.maximum(top, carried)
        a = jnp.exp(top - row_max)
        b = jnp.exp(carried - row_max) * factor
        den = a * inner_den + b * cross_den
        inverse = 1.0 / jnp.maximum(jnp.abs(den), jnp.exp(jnp.maximum(-row_max, 0.0)))
        hidden = (a * inverse) * inner + (b * inverse) * cross
        out_ref[0, :, h * dv:(h + 1) * dv] = hidden.astype(jnp.bfloat16)

    @pl.when(z < Z - 1)
    def _():
        info_copy().wait_send()
        for h in range(heads):
            mem_copy(h).wait_send()

    if spread:
        def drain(s, carry):
            zz, p = s // pieces, s % pieces

            @pl.when(jnp.logical_and(z < Z - 1, zz <= z))
            def _():
                z_copy(0, zz, p).wait_send()

            @pl.when(jnp.logical_and(z > 0, zz >= z))
            def _():
                z_copy(1, zz, p).wait_send()

            x_copy(x, zz, p).wait_send()

            @pl.when(zz != z)
            def _():
                y_copy(x, zz, p, 1).wait_send()

            y_copy(1 - x, zz, p, 1).wait_send()
            for xx in (x, 1 - x):
                for part in (0, 2):
                    c_copy(xx, c, zz, p, part).wait_send()
            return carry

        lax.fori_loop(0, Z * pieces, drain, 0)


def body(Z, dp, planes, normed_input, query_weight, key_vectors, value_vectors, input_gate, forget_gate, resets):
    _, length, features = normed_input.shape
    heads = input_gate.shape[1]
    width = query_weight.shape[1]
    dk = key_vectors.shape[2] // heads
    dv = value_vectors.shape[2] // heads
    spread = dp == 4 and planes == 2 and query_weight.shape[0] % 256 == 0
    if spread:
        rows = query_weight.shape[0]
        weight = query_weight
    else:
        rows = 256
        weight = lax.all_gather(query_weight, ("dp", "ctx"), axis=0, tiled=True)
    count = features // rows if spread else 1
    dma = pltpu.SemaphoreType.DMA
    hbm = pl.BlockSpec(memory_space=pltpu.HBM)
    vmem = pl.BlockSpec(memory_space=pltpu.VMEM)
    return pl.pallas_call(
        functools.partial(kernel, spread, Z, heads),
        out_shape=jax.ShapeDtypeStruct((1, length, heads * dv), jnp.bfloat16),
        in_specs=[hbm] * 7,
        out_specs=vmem,
        scratch_shapes=[
            pltpu.VMEM((2, 8, length), jnp.float32),
            pltpu.VMEM((1, length), jnp.int32),
            pltpu.VMEM((length, features), jnp.bfloat16),
            pltpu.VMEM((length, heads * dk), jnp.bfloat16),
            pltpu.VMEM((length, heads * dv), jnp.bfloat16),
            pltpu.VMEM(weight.shape, jnp.bfloat16),
            pltpu.VMEM((count, rows, width), jnp.bfloat16),
            pltpu.VMEM((length, width), jnp.float32),
            pltpu.VMEM((heads, length, length), jnp.float32),
            pltpu.VMEM((128, length), jnp.float32),
            pltpu.VMEM((length, 128), jnp.float32),
            pltpu.VMEM((length, 128), jnp.float32),
            pltpu.VMEM((heads, dk, dv), jnp.float32),
            pltpu.VMEM((2 * heads, dk), jnp.float32),
            pltpu.VMEM((heads, dk, dv), jnp.bfloat16),
            pltpu.VMEM((2 * heads, dk), jnp.float32),
            pltpu.VMEM((heads, dk, dv), jnp.bfloat16),
            pltpu.VMEM((2 * heads, dk), jnp.float32),
            dma((7,)),
            dma((2, Z, pieces)), dma((Z, pieces)),
            dma((Z, pieces)), dma((Z, pieces)),
            dma((2, Z, pieces)), dma((2, Z, pieces)),
            dma((2, Z, pieces, 2)), dma((2, Z, pieces, 2)),
            dma((heads + 1,)), dma((heads + 1,)),
        ],
        compiler_params=pltpu.CompilerParams(
            collective_id=0, has_side_effects=True, vmem_limit_bytes=60 * 1024 * 1024
        ),
        cost_estimate=pl.CostEstimate(
            flops=2 * length * features * width, bytes_accessed=6 * 1024 * 1024, transcendentals=0
        ),
    )(normed_input, weight, key_vectors, value_vectors, input_gate, forget_gate, resets)


def solution(mesh):
    sizes = mesh.shape
    return jax.shard_map(
        functools.partial(body, sizes["ctx"], sizes["dp"], sizes["groups"]),
        mesh=mesh,
        in_specs=(
            P(("groups", "dp"), "ctx", None),
            P(("dp", "ctx"), None),
            P(("groups", "dp"), "ctx", None),
            P(("groups", "dp"), "ctx", None),
            P(("groups", "dp"), None, "ctx"),
            P(("groups", "dp"), None, "ctx"),
            P(("groups", "dp"), "ctx"),
        ),
        out_specs=P(("groups", "dp"), "ctx", None),
        check_vma=False,
    )
```

```python
import functools

import jax
import jax.numpy as jnp
from jax import lax
from jax.experimental import pallas as pl
from jax.experimental.pallas import tpu as pltpu
from jax.sharding import PartitionSpec as P

very_low = -1e30
shared_columns = 256
pieces = 2
MESH = pl.DeviceIdType.MESH


def dot(a, b, dims=((1,), (0,))):
    return lax.dot_general(a, b, (dims, ((), ())), preferred_element_type=jnp.float32)


def kernel(
    spread, Z, heads, x_hbm, w_hbm, k_hbm, v_hbm, ig_hbm, fg_hbm, rs_hbm, out_ref,
    gates, flags, xv, kv, vv, wown, wbuf, acc, prob, stack, cols, imax_scr, own_mem, own_info,
    mem_in, info_in, mem_out, info_out,
    lsem, zsend, zrecv, xsend, xrecv, ysend, yrecv, csend, crecv, ssend, srecv,
):
    y = lax.axis_index("groups")
    d = lax.axis_index("dp")
    z = lax.axis_index("ctx")
    x, c = d // 2, d % 2
    up, down = (y, d, z + 1), (y, d, z - 1)
    across = (y, (1 - x) * 2 + c, z)
    over = (1 - y, d, z)
    mate = (y, x * 2 + 1 - c, z)
    length, features = xv.shape
    dk = kv.shape[1] // heads
    dv = vv.shape[1] // heads
    factor = dk ** (-0.5)
    width = acc.shape[1]
    rows = wbuf.shape[1]
    A = shared_columns

    local = [
        pltpu.make_async_copy(ig_hbm.at[0], gates.at[0, 0:heads], lsem.at[4]),
        pltpu.make_async_copy(fg_hbm.at[0], gates.at[1, 0:heads], lsem.at[5]),
        pltpu.make_async_copy(rs_hbm, flags, lsem.at[6]),
        pltpu.make_async_copy(k_hbm.at[0], kv, lsem.at[0]),
        pltpu.make_async_copy(v_hbm.at[0], vv, lsem.at[1]),
        pltpu.make_async_copy(x_hbm.at[0], xv, lsem.at[2]),
        pltpu.make_async_copy(w_hbm, wown, lsem.at[3]),
    ]
    for one in local:
        one.start()

    barrier = pltpu.get_barrier_semaphore()

    def greet(device):
        pl.semaphore_signal(barrier, inc=1, device_id=device, device_id_type=MESH)

    @pl.when(z < Z - 1)
    def _():
        greet(up)

    @pl.when(z > 0)
    def _():
        greet(down)

    base = 0
    if spread:
        for device in (across, over, mate):
            greet(device)
        base = 3
    pl.semaphore_wait(
        barrier, base + jnp.where(z > 0, 1, 0) + jnp.where(z < Z - 1, 1, 0)
    )

    B = width - 2 * A

    def columns(part):
        if part == 0:
            return pl.ds(pl.multiple_of(y * A, 128), A + B)
        if part == 1:
            return pl.ds(pl.multiple_of(y * (A + B), 128), A)
        return pl.ds(pl.multiple_of((1 - y) * (A + B), 128), A)

    high = rows // pieces

    def shard(xx, cc, zz):
        return (xx * 2 + cc) * Z + zz

    def remote(xx, cc, zz, p, part, send, recv, device, own=False):
        at = pl.ds(p * high if isinstance(p, int) else pl.multiple_of(p * high, 16), high)
        there = wbuf.at[shard(xx, cc, zz), at, columns(part)]
        here = w_hbm.at[at, columns(part)] if own else there
        return pltpu.make_async_remote_copy(
            src_ref=here, dst_ref=there, send_sem=send, recv_sem=recv,
            device_id=device, device_id_type=MESH,
        )

    def z_copy(way, zz, p, own=False):
        device = up if way == 0 else down
        return remote(x, c, zz, p, 0, zsend.at[way, zz, p], zrecv.at[zz, p], device, own)

    def x_copy(xx, zz, p, own=False):
        return remote(xx, c, zz, p, 0, xsend.at[zz, p], xrecv.at[zz, p], across, own)

    def y_copy(xx, zz, p, part):
        return remote(xx, c, zz, p, part, ysend.at[xx, zz, p], yrecv.at[xx, zz, p], over)

    def c_copy(xx, cc, zz, p, part, own=False):
        return remote(
            xx, cc, zz, p, part, csend.at[xx, zz, p, part // 2], crecv.at[xx, zz, p, part // 2], mate, own
        )

    if spread:
        for p in range(pieces):
            @pl.when(z < Z - 1)
            def _():
                z_copy(0, z, p, True).start()

            @pl.when(z > 0)
            def _():
                z_copy(1, z, p, True).start()

            x_copy(x, z, p, True).start()
        for p in range(pieces):
            for part in (0, 2):
                c_copy(x, c, z, p, part, True).start()

    for one in local[:3]:
        one.wait()

    f = gates[1, 0:heads, :]
    stack[...] = jnp.zeros_like(stack)
    stack[0:heads, :] = jnp.minimum(f, 0.0) - jnp.log1p(jnp.exp(-jnp.abs(f)))
    stack[4:5, :] = flags[...].astype(jnp.float32)
    run = stack[0:8, :]
    lane = lax.broadcasted_iota(jnp.int32, run.shape, 1)
    hop = 1
    while hop < length:
        run = run + jnp.where(lane >= hop, pltpu.roll(run, hop, 1), 0.0)
        hop *= 2
    stack[0:8, :] = run
    stack[8:8 + heads, :] = gates[0, 0:heads, :]
    cols[...] = stack[...].T

    def row(at):
        return stack[at:at + 1, :]

    def col(at):
        return cols[:, at:at + 1]

    def last(at):
        return stack[at:at + 1, length - 1:length]

    def own_state(h):
        end_row = jnp.where(row(4) == last(4), last(h) - row(h) + row(8 + h), very_low)
        top = jnp.max(end_row, axis=1, keepdims=True)
        end_col = jnp.where(col(4) == last(4), last(h) - col(h) + col(8 + h), very_low)
        weighted = (
            kv[:, h * dk:(h + 1) * dk].astype(jnp.float32) * jnp.exp(end_col - top)
        ).astype(jnp.bfloat16)
        own_mem[h] = dot(weighted, vv[:, h * dv:(h + 1) * dv], ((0,), (0,)))
        own_info[h:h + 1, :] = jnp.sum(weighted.astype(jnp.float32), axis=0, keepdims=True)
        own_info[heads + h:heads + h + 1, :] = jnp.broadcast_to(top, (1, dk))

    def decay(h):
        row_at = lax.broadcasted_iota(jnp.int32, (length, length), 0)
        col_at = lax.broadcasted_iota(jnp.int32, (length, length), 1)
        linked = jnp.logical_and(col(4) == row(4), row_at >= col_at)
        exponent = jnp.where(linked, col(h) - row(h) + row(8 + h), very_low)
        top = jnp.max(exponent, axis=1, keepdims=True)
        imax_scr[:, h:h + 1] = top
        prob[h] = jnp.exp(exponent - top) * factor

    def info_copy():
        return pltpu.make_async_remote_copy(
            src_ref=info_out, dst_ref=info_in, send_sem=ssend.at[heads], recv_sem=srecv.at[heads],
            device_id=up, device_id_type=MESH,
        )

    def mem_copy(h):
        return pltpu.make_async_remote_copy(
            src_ref=mem_out.at[h], dst_ref=mem_in.at[h], send_sem=ssend.at[h], recv_sem=srecv.at[h],
            device_id=up, device_id_type=MESH,
        )

    def pass_head(h):
        if h == 0:
            @pl.when(z > 0)
            def _():
                info_copy().wait_recv()

        @pl.when(z > 0)
        def _():
            mem_copy(h).wait_recv()

        @pl.when(z < Z - 1)
        def _():
            def blend(at):
                gap = jnp.where(last(4) > 0, very_low, last(at))
                shifted = info_in[heads + at:heads + at + 1, :] + gap
                top = own_info[heads + at:heads + at + 1, :]
                both = jnp.maximum(shifted, top)
                return both, jnp.exp(shifted - both), jnp.exp(top - both)

            if h == 0:
                for at in range(heads):
                    both, early, late = blend(at)
                    info_out[at:at + 1, :] = early * info_in[at:at + 1, :] + late * own_info[at:at + 1, :]
                    info_out[heads + at:heads + at + 1, :] = both
                info_copy().start()
            _, early, late = blend(h)
            mem_out[h] = (
                early[:, 0:1] * mem_in[h].astype(jnp.float32) + late[:, 0:1] * own_mem[h]
            ).astype(jnp.bfloat16)
            mem_copy(h).start()

    def start_state():
        for one in local[3:5]:
            one.wait()
        for h in range(heads):
            own_state(h)

        @pl.when(z == 0)
        def _():
            mem_in[...] = jnp.zeros_like(mem_in)
            info_in[0:heads, :] = jnp.zeros((heads, dk), jnp.float32)
            info_in[heads:, :] = jnp.full((heads, dk), very_low, jnp.float32)
            for h in range(heads):
                pass_head(h)

    if not spread:
        start_state()

        @pl.when(z > 0)
        def _():
            for h in range(heads):
                pass_head(h)

        for h in range(heads):
            decay(h)
        for one in local[5:]:
            one.wait()

    def multiply(at, piece):
        part = xv[:, pl.ds(pl.multiple_of(at * rows, 128), rows)]
        acc[...] += dot(part, piece)

    if spread:
        state_steps = [-(-2 * pieces * (h + 1) // 5) for h in range(heads)]
        def places(s, low):
            q = (s + pieces) // pieces - 1
            p = (s + pieces) % pieces
            below, above = z - q, z + q
            yield below, p, jnp.logical_and(q >= low, jnp.logical_and(q < Z, below >= 0))
            yield above, p, jnp.logical_and(q >= max(low, 1), above < Z)

        def take(xx, cc, zz, p):
            @pl.when(p == pieces - 1)
            def _():
                multiply(shard(xx, cc, zz), wbuf[shard(xx, cc, zz)])

        def one_step(t, carry):
            for way, (zz, p, ok) in enumerate(places(t, 1)):
                @pl.when(ok)
                def _():
                    z_copy(way, zz, p).wait_recv()

                    @pl.when(z < Z - 1 if way == 0 else z > 0)
                    def _():
                        z_copy(way, zz, p).start()

                    x_copy(x, zz, p).start()
                    y_copy(x, zz, p, 1).start()
                    c_copy(x, c, zz, p, 0).start()

            for zz, p, ok in places(t - 1, 0):
                @pl.when(ok)
                def _():
                    x_copy(1 - x, zz, p).wait_recv()
                    y_copy(1 - x, zz, p, 1).start()
                    c_copy(1 - x, c, zz, p, 0).start()

            for h in range(heads):
                @pl.when(jnp.logical_and(t == z * pieces + state_steps[h], jnp.logical_and(z > 0, z < Z - 1)))
                def _():
                    pass_head(h)

            @pl.when(t == 1)
            def _():
                start_state()
                for one in local[5:]:
                    one.wait()
                acc[...] = dot(
                    xv[:, pl.ds(pl.multiple_of(shard(x, c, z) * rows, 128), rows)], wown[...]
                )

            for h in range(heads):
                @pl.when(t == pieces + 1 + h * (pieces // 2))
                def _():
                    decay(h)

            for zz, p, ok in places(t - 1, 1):
                @pl.when(ok)
                def _():
                    y_copy(x, zz, p, 2).wait_recv()
                    c_copy(x, c, zz, p, 2).start()
                    take(x, c, zz, p)

            for zz, p, ok in places(t - 2, 0):
                @pl.when(ok)
                def _():
                    y_copy(1 - x, zz, p, 2).wait_recv()
                    c_copy(1 - x, c, zz, p, 2).start()
                    take(1 - x, c, zz, p)

                @pl.when(ok)
                def _():
                    for part in (0, 2):
                        c_copy(x, 1 - c, zz, p, part).wait_recv()
                    take(x, 1 - c, zz, p)

            for zz, p, ok in places(t - 3, 0):
                @pl.when(ok)
                def _():
                    for part in (0, 2):
                        c_copy(1 - x, 1 - c, zz, p, part).wait_recv()
                    take(1 - x, 1 - c, zz, p)

            return carry

        lax.fori_loop(1, Z * pieces + 3, one_step, 0)

        @pl.when(z == Z - 1)
        def _():
            for h in range(heads):
                pass_head(h)

    else:
        acc[...] = jnp.zeros_like(acc)

        def one_block(at, carry):
            multiply(at, wown[pl.ds(pl.multiple_of(at * rows, 16), rows), :])
            return carry

        lax.fori_loop(0, features // rows, one_block, 0)

    info = info_in[...]
    for h in range(heads):
        q = acc[:, h * dk:(h + 1) * dk].astype(jnp.bfloat16)
        values = vv[:, h * dv:(h + 1) * dv]
        scores = dot(q, kv[:, h * dk:(h + 1) * dk], ((1,), (1,)))
        weighted = (scores * prob[h]).astype(jnp.bfloat16)
        inner = dot(weighted, values)
        inner_den = jnp.sum(weighted.astype(jnp.float32), axis=1, keepdims=True)
        cross = dot(q, mem_in[h])
        normer = info[h:h + 1, :].astype(jnp.bfloat16).astype(jnp.float32)
        cross_den = jnp.sum(q.astype(jnp.float32) * normer, axis=1, keepdims=True)
        top = imax_scr[:, h:h + 1]
        carried = jnp.where(col(4) == 0, col(h) + info[heads + h:heads + h + 1, 0:1], very_low)
        row_max = jnp.maximum(top, carried)
        a = jnp.exp(top - row_max)
        b = jnp.exp(carried - row_max) * factor
        den = a * inner_den + b * cross_den
        inverse = 1.0 / jnp.maximum(jnp.abs(den), jnp.exp(jnp.maximum(-row_max, 0.0)))
        hidden = (a * inverse) * inner + (b * inverse) * cross
        out_ref[0, :, h * dv:(h + 1) * dv] = hidden.astype(jnp.bfloat16)

    @pl.when(z < Z - 1)
    def _():
        info_copy().wait_send()
        for h in range(heads):
            mem_copy(h).wait_send()

    if spread:
        def drain(s, carry):
            zz, p = s // pieces, s % pieces

            @pl.when(jnp.logical_and(z < Z - 1, zz <= z))
            def _():
                z_copy(0, zz, p).wait_send()

            @pl.when(jnp.logical_and(z > 0, zz >= z))
            def _():
                z_copy(1, zz, p).wait_send()

            x_copy(x, zz, p).wait_send()

            @pl.when(zz != z)
            def _():
                y_copy(x, zz, p, 1).wait_send()

            y_copy(1 - x, zz, p, 1).wait_send()
            for xx in (x, 1 - x):
                for part in (0, 2):
                    c_copy(xx, c, zz, p, part).wait_send()
            return carry

        lax.fori_loop(0, Z * pieces, drain, 0)


def body(Z, dp, planes, normed_input, query_weight, key_vectors, value_vectors, input_gate, forget_gate, resets):
    _, length, features = normed_input.shape
    heads = input_gate.shape[1]
    width = query_weight.shape[1]
    dk = key_vectors.shape[2] // heads
    dv = value_vectors.shape[2] // heads
    spread = dp == 4 and planes == 2 and query_weight.shape[0] % 256 == 0
    if spread:
        rows = query_weight.shape[0]
        weight = query_weight
    else:
        rows = 256
        weight = lax.all_gather(query_weight, ("dp", "ctx"), axis=0, tiled=True)
    count = features // rows if spread else 1
    dma = pltpu.SemaphoreType.DMA
    hbm = pl.BlockSpec(memory_space=pltpu.HBM)
    vmem = pl.BlockSpec(memory_space=pltpu.VMEM)
    return pl.pallas_call(
        functools.partial(kernel, spread, Z, heads),
        out_shape=jax.ShapeDtypeStruct((1, length, heads * dv), jnp.bfloat16),
        in_specs=[hbm] * 7,
        out_specs=vmem,
        scratch_shapes=[
            pltpu.VMEM((2, 8, length), jnp.float32),
            pltpu.VMEM((1, length), jnp.int32),
            pltpu.VMEM((length, features), jnp.bfloat16),
            pltpu.VMEM((length, heads * dk), jnp.bfloat16),
            pltpu.VMEM((length, heads * dv), jnp.bfloat16),
            pltpu.VMEM(weight.shape, jnp.bfloat16),
            pltpu.VMEM((count, rows, width), jnp.bfloat16),
            pltpu.VMEM((length, width), jnp.float32),
            pltpu.VMEM((heads, length, length), jnp.float32),
            pltpu.VMEM((128, length), jnp.float32),
            pltpu.VMEM((length, 128), jnp.float32),
            pltpu.VMEM((length, 128), jnp.float32),
            pltpu.VMEM((heads, dk, dv), jnp.float32),
            pltpu.VMEM((2 * heads, dk), jnp.float32),
            pltpu.VMEM((heads, dk, dv), jnp.bfloat16),
            pltpu.VMEM((2 * heads, dk), jnp.float32),
            pltpu.VMEM((heads, dk, dv), jnp.bfloat16),
            pltpu.VMEM((2 * heads, dk), jnp.float32),
            dma((7,)),
            dma((2, Z, pieces)), dma((Z, pieces)),
            dma((Z, pieces)), dma((Z, pieces)),
            dma((2, Z, pieces)), dma((2, Z, pieces)),
            dma((2, Z, pieces, 2)), dma((2, Z, pieces, 2)),
            dma((heads + 1,)), dma((heads + 1,)),
        ],
        compiler_params=pltpu.CompilerParams(
            collective_id=0, has_side_effects=True, vmem_limit_bytes=60 * 1024 * 1024
        ),
        cost_estimate=pl.CostEstimate(
            flops=2 * length * features * width, bytes_accessed=6 * 1024 * 1024, transcendentals=0
        ),
    )(normed_input, weight, key_vectors, value_vectors, input_gate, forget_gate, resets)


def solution(mesh):
    sizes = mesh.shape
    return jax.shard_map(
        functools.partial(body, sizes["ctx"], sizes["dp"], sizes["groups"]),
        mesh=mesh,
        in_specs=(
            P(("groups", "dp"), "ctx", None),
            P(("dp", "ctx"), None),
            P(("groups", "dp"), "ctx", None),
            P(("groups", "dp"), "ctx", None),
            P(("groups", "dp"), None, "ctx"),
            P(("groups", "dp"), None, "ctx"),
            P(("groups", "dp"), "ctx"),
        ),
        out_specs=P(("groups", "dp"), "ctx", None),
        check_vma=False,
    )
```

```python
import functools

import jax
import jax.numpy as jnp
from jax import lax
from jax.experimental import pallas as pl
from jax.experimental.pallas import tpu as pltpu
from jax.sharding import PartitionSpec as P

very_low = -1e30
shared_columns = 384
pieces = 4
lag_across, lag_over, lag_over_across, lag_mate, lag_mate_across = 2, 2, 4, 5, 7
MESH = pl.DeviceIdType.MESH


def dot(a, b, dims=((1,), (0,))):
    return lax.dot_general(a, b, (dims, ((), ())), preferred_element_type=jnp.float32)


def kernel(
    spread, Z, heads, x_hbm, w_hbm, k_hbm, v_hbm, ig_hbm, fg_hbm, rs_hbm, out_ref,
    gates, flags, xv, kv, vv, wown, wbuf, acc, prob, stack, cols, imax_scr, own_mem, own_info,
    mem_in, info_in, mem_out, info_out,
    lsem, zsend, zrecv, xsend, xrecv, ysend, yrecv, csend, crecv, ssend, srecv,
):
    y = lax.axis_index("groups")
    d = lax.axis_index("dp")
    z = lax.axis_index("ctx")
    x, c = d // 2, d % 2
    up, down = (y, d, z + 1), (y, d, z - 1)
    across = (y, (1 - x) * 2 + c, z)
    over = (1 - y, d, z)
    mate = (y, x * 2 + 1 - c, z)
    length, features = xv.shape
    dk = kv.shape[1] // heads
    dv = vv.shape[1] // heads
    factor = dk ** (-0.5)
    width = acc.shape[1]
    rows = wbuf.shape[1]
    A = shared_columns

    local = [
        pltpu.make_async_copy(ig_hbm.at[0], gates.at[0, 0:heads], lsem.at[4]),
        pltpu.make_async_copy(fg_hbm.at[0], gates.at[1, 0:heads], lsem.at[5]),
        pltpu.make_async_copy(rs_hbm, flags, lsem.at[6]),
        pltpu.make_async_copy(k_hbm.at[0], kv, lsem.at[0]),
        pltpu.make_async_copy(v_hbm.at[0], vv, lsem.at[1]),
        pltpu.make_async_copy(x_hbm.at[0], xv, lsem.at[2]),
        pltpu.make_async_copy(w_hbm, wown, lsem.at[3]),
    ]
    for one in local:
        one.start()

    barrier = pltpu.get_barrier_semaphore()

    def greet(device):
        pl.semaphore_signal(barrier, inc=1, device_id=device, device_id_type=MESH)

    @pl.when(z < Z - 1)
    def _():
        greet(up)

    @pl.when(z > 0)
    def _():
        greet(down)

    base = 0
    if spread:
        for device in (across, over, mate):
            greet(device)
        base = 3
    pl.semaphore_wait(
        barrier, base + jnp.where(z > 0, 1, 0) + jnp.where(z < Z - 1, 1, 0)
    )

    B = width - 2 * A

    def columns(part):
        if part == 0:
            return pl.ds(pl.multiple_of(y * A, 128), A + B)
        if part == 1:
            return pl.ds(pl.multiple_of(y * (A + B), 128), A)
        return pl.ds(pl.multiple_of((1 - y) * (A + B), 128), A)

    high = rows // pieces

    def shard(xx, cc, zz):
        return (xx * 2 + cc) * Z + zz

    def remote(xx, cc, zz, p, part, send, recv, device, own=False):
        at = pl.ds(p * high if isinstance(p, int) else pl.multiple_of(p * high, 16), high)
        there = wbuf.at[shard(xx, cc, zz), at, columns(part)]
        here = w_hbm.at[at, columns(part)] if own else there
        return pltpu.make_async_remote_copy(
            src_ref=here, dst_ref=there, send_sem=send, recv_sem=recv,
            device_id=device, device_id_type=MESH,
        )

    def z_copy(way, zz, p, own=False):
        device = up if way == 0 else down
        return remote(x, c, zz, p, 0, zsend.at[way], zrecv.at[zz, p], device, own)

    def x_copy(xx, zz, p, own=False):
        return remote(xx, c, zz, p, 0, xsend.at[0], xrecv.at[zz, p], across, own)

    def y_copy(xx, zz, p, part):
        return remote(xx, c, zz, p, part, ysend.at[xx], yrecv.at[xx, zz, p], over)

    def c_copy(xx, cc, zz, p, part, own=False):
        return remote(
            xx, cc, zz, p, part, csend.at[0], crecv.at[xx, zz, p, part // 2], mate, own
        )

    if spread:
        for p in range(pieces):
            @pl.when(z < Z - 1)
            def _():
                z_copy(0, z, p, True).start()

            @pl.when(z > 0)
            def _():
                z_copy(1, z, p, True).start()

            x_copy(x, z, p, True).start()
        for p in range(pieces):
            for part in (0, 2):
                c_copy(x, c, z, p, part, True).start()

    for one in local[:3]:
        one.wait()

    f = gates[1, 0:heads, :]
    stack[...] = jnp.zeros_like(stack)
    stack[0:heads, :] = jnp.minimum(f, 0.0) - jnp.log1p(jnp.exp(-jnp.abs(f)))
    stack[4:5, :] = flags[...].astype(jnp.float32)
    run = stack[0:8, :]
    lane = lax.broadcasted_iota(jnp.int32, run.shape, 1)
    hop = 1
    while hop < length:
        run = run + jnp.where(lane >= hop, pltpu.roll(run, hop, 1), 0.0)
        hop *= 2
    stack[0:8, :] = run
    stack[8:8 + heads, :] = gates[0, 0:heads, :]
    cols[...] = stack[...].T

    def row(at):
        return stack[at:at + 1, :]

    def col(at):
        return cols[:, at:at + 1]

    def last(at):
        return stack[at:at + 1, length - 1:length]

    def own_state(h):
        end_row = jnp.where(row(4) == last(4), last(h) - row(h) + row(8 + h), very_low)
        top = jnp.max(end_row, axis=1, keepdims=True)
        end_col = jnp.where(col(4) == last(4), last(h) - col(h) + col(8 + h), very_low)
        weighted = (
            kv[:, h * dk:(h + 1) * dk].astype(jnp.float32) * jnp.exp(end_col - top)
        ).astype(jnp.bfloat16)
        own_mem[h] = dot(weighted, vv[:, h * dv:(h + 1) * dv], ((0,), (0,)))
        own_info[h:h + 1, :] = jnp.sum(weighted.astype(jnp.float32), axis=0, keepdims=True)
        own_info[heads + h:heads + h + 1, :] = jnp.broadcast_to(top, (1, dk))

    def decay(h):
        row_at = lax.broadcasted_iota(jnp.int32, (length, length), 0)
        col_at = lax.broadcasted_iota(jnp.int32, (length, length), 1)
        linked = jnp.logical_and(col(4) == row(4), row_at >= col_at)
        exponent = jnp.where(linked, col(h) - row(h) + row(8 + h), very_low)
        top = jnp.max(exponent, axis=1, keepdims=True)
        imax_scr[:, h:h + 1] = top
        prob[h] = jnp.exp(exponent - top) * factor

    def info_copy():
        return pltpu.make_async_remote_copy(
            src_ref=info_out, dst_ref=info_in, send_sem=ssend.at[heads], recv_sem=srecv.at[heads],
            device_id=up, device_id_type=MESH,
        )

    def mem_copy(h):
        return pltpu.make_async_remote_copy(
            src_ref=mem_out.at[h], dst_ref=mem_in.at[h], send_sem=ssend.at[h], recv_sem=srecv.at[h],
            device_id=up, device_id_type=MESH,
        )

    def pass_head(h):
        if h == 0:
            @pl.when(z > 0)
            def _():
                info_copy().wait_recv()

        @pl.when(z > 0)
        def _():
            mem_copy(h).wait_recv()

        @pl.when(z < Z - 1)
        def _():
            def blend(at):
                gap = jnp.where(last(4) > 0, very_low, last(at))
                shifted = info_in[heads + at:heads + at + 1, :] + gap
                top = own_info[heads + at:heads + at + 1, :]
                both = jnp.maximum(shifted, top)
                return both, jnp.exp(shifted - both), jnp.exp(top - both)

            if h == 0:
                for at in range(heads):
                    both, early, late = blend(at)
                    info_out[at:at + 1, :] = early * info_in[at:at + 1, :] + late * own_info[at:at + 1, :]
                    info_out[heads + at:heads + at + 1, :] = both
                info_copy().start()
            _, early, late = blend(h)
            mem_out[h] = (
                early[:, 0:1] * mem_in[h].astype(jnp.float32) + late[:, 0:1] * own_mem[h]
            ).astype(jnp.bfloat16)
            mem_copy(h).start()

    def start_state():
        for one in local[3:5]:
            one.wait()
        for h in range(heads):
            own_state(h)

        @pl.when(z == 0)
        def _():
            mem_in[...] = jnp.zeros_like(mem_in)
            info_in[0:heads, :] = jnp.zeros((heads, dk), jnp.float32)
            info_in[heads:, :] = jnp.full((heads, dk), very_low, jnp.float32)
            for h in range(heads):
                pass_head(h)

    if not spread:
        start_state()

        @pl.when(z > 0)
        def _():
            for h in range(heads):
                pass_head(h)

        for h in range(heads):
            decay(h)
        for one in local[5:]:
            one.wait()

    def multiply(at, piece):
        part = xv[:, pl.ds(pl.multiple_of(at * rows, 128), rows)]
        acc[...] += dot(part, piece)

    if spread:
        state_steps = [-(-2 * pieces * (h + 1) // 5) for h in range(heads)]
        def places(s, low):
            q = (s + 2 * pieces) // pieces - 2
            p = (s + 2 * pieces) % pieces
            below, above = z - q, z + q
            yield below, p, jnp.logical_and(q >= low, jnp.logical_and(q < Z, below >= 0))
            yield above, p, jnp.logical_and(q >= max(low, 1), above < Z)

        def take(xx, cc, zz, p):
            @pl.when(p == pieces - 1)
            def _():
                multiply(shard(xx, cc, zz), wbuf[shard(xx, cc, zz)])

        def one_step(t, carry):
            for way, (zz, p, ok) in enumerate(places(t, 1)):
                @pl.when(ok)
                def _():
                    z_copy(way, zz, p).wait_recv()

                    @pl.when(z < Z - 1 if way == 0 else z > 0)
                    def _():
                        z_copy(way, zz, p).start()

                    x_copy(x, zz, p).start()
                    y_copy(x, zz, p, 1).start()
                    c_copy(x, c, zz, p, 0).start()

            for zz, p, ok in places(t - lag_across, 0):
                @pl.when(ok)
                def _():
                    x_copy(1 - x, zz, p).wait_recv()
                    y_copy(1 - x, zz, p, 1).start()
                    c_copy(1 - x, c, zz, p, 0).start()

            for h in range(heads):
                @pl.when(jnp.logical_and(t == z * pieces + state_steps[h], jnp.logical_and(z > 0, z < Z - 1)))
                def _():
                    pass_head(h)

            @pl.when(t == lag_across + 1)
            def _():
                start_state()
                for one in local[5:]:
                    one.wait()
                acc[...] = dot(
                    xv[:, pl.ds(pl.multiple_of(shard(x, c, z) * rows, 128), rows)], wown[...]
                )

            for h in range(heads):
                @pl.when(t == pieces + 1 + h * (pieces // 2))
                def _():
                    decay(h)

            for zz, p, ok in places(t - lag_over, 1):
                @pl.when(ok)
                def _():
                    y_copy(x, zz, p, 2).wait_recv()
                    c_copy(x, c, zz, p, 2).start()
                    take(x, c, zz, p)

            for zz, p, ok in places(t - lag_over_across, 0):
                @pl.when(ok)
                def _():
                    y_copy(1 - x, zz, p, 2).wait_recv()
                    c_copy(1 - x, c, zz, p, 2).start()
                    take(1 - x, c, zz, p)

            for zz, p, ok in places(t - lag_mate, 0):
                @pl.when(ok)
                def _():
                    for part in (0, 2):
                        c_copy(x, 1 - c, zz, p, part).wait_recv()
                    take(x, 1 - c, zz, p)

            for zz, p, ok in places(t - lag_mate_across, 0):
                @pl.when(ok)
                def _():
                    for part in (0, 2):
                        c_copy(1 - x, 1 - c, zz, p, part).wait_recv()
                    take(1 - x, 1 - c, zz, p)

            return carry

        lax.fori_loop(1, Z * pieces + lag_mate_across, one_step, 0)

        @pl.when(z == Z - 1)
        def _():
            for h in range(heads):
                pass_head(h)

    else:
        acc[...] = jnp.zeros_like(acc)

        def one_block(at, carry):
            multiply(at, wown[pl.ds(pl.multiple_of(at * rows, 16), rows), :])
            return carry

        lax.fori_loop(0, features // rows, one_block, 0)

    info = info_in[...]
    for h in range(heads):
        q = acc[:, h * dk:(h + 1) * dk].astype(jnp.bfloat16)
        values = vv[:, h * dv:(h + 1) * dv]
        scores = dot(q, kv[:, h * dk:(h + 1) * dk], ((1,), (1,)))
        weighted = (scores * prob[h]).astype(jnp.bfloat16)
        inner = dot(weighted, values)
        inner_den = jnp.sum(weighted.astype(jnp.float32), axis=1, keepdims=True)
        cross = dot(q, mem_in[h])
        normer = info[h:h + 1, :].astype(jnp.bfloat16).astype(jnp.float32)
        cross_den = jnp.sum(q.astype(jnp.float32) * normer, axis=1, keepdims=True)
        top = imax_scr[:, h:h + 1]
        carried = jnp.where(col(4) == 0, col(h) + info[heads + h:heads + h + 1, 0:1], very_low)
        row_max = jnp.maximum(top, carried)
        a = jnp.exp(top - row_max)
        b = jnp.exp(carried - row_max) * factor
        den = a * inner_den + b * cross_den
        inverse = 1.0 / jnp.maximum(jnp.abs(den), jnp.exp(jnp.maximum(-row_max, 0.0)))
        hidden = (a * inverse) * inner + (b * inverse) * cross
        out_ref[0, :, h * dv:(h + 1) * dv] = hidden.astype(jnp.bfloat16)

    @pl.when(z < Z - 1)
    def _():
        info_copy().wait_send()
        for h in range(heads):
            mem_copy(h).wait_send()

    if spread:
        def drain(sem, count, wide):
            some = wbuf.at[0:count, :, 0:wide]
            pltpu.make_async_remote_copy(
                src_ref=some, dst_ref=some, send_sem=sem, recv_sem=sem, device_id=mate, device_id_type=MESH
            ).wait_send()

        for at in range(Z):
            @pl.when(z == at)
            def _():
                if at < Z - 1:
                    drain(zsend.at[0], at + 1, A + B)
                if at > 0:
                    drain(zsend.at[1], Z - at, A + B)

        drain(xsend.at[0], Z, A + B)
        drain(ysend.at[x], Z - 1, A)
        drain(ysend.at[1 - x], Z, A)
        drain(csend.at[0], 2 * Z, width)


def body(Z, dp, planes, normed_input, query_weight, key_vectors, value_vectors, input_gate, forget_gate, resets):
    _, length, features = normed_input.shape
    heads = input_gate.shape[1]
    width = query_weight.shape[1]
    dk = key_vectors.shape[2] // heads
    dv = value_vectors.shape[2] // heads
    spread = dp == 4 and planes == 2 and query_weight.shape[0] % 256 == 0
    if spread:
        rows = query_weight.shape[0]
        weight = query_weight
    else:
        rows = 256
        weight = lax.all_gather(query_weight, ("dp", "ctx"), axis=0, tiled=True)
    count = features // rows if spread else 1
    dma = pltpu.SemaphoreType.DMA
    hbm = pl.BlockSpec(memory_space=pltpu.HBM)
    vmem = pl.BlockSpec(memory_space=pltpu.VMEM)
    return pl.pallas_call(
        functools.partial(kernel, spread, Z, heads),
        out_shape=jax.ShapeDtypeStruct((1, length, heads * dv), jnp.bfloat16),
        in_specs=[hbm] * 7,
        out_specs=vmem,
        scratch_shapes=[
            pltpu.VMEM((2, 8, length), jnp.float32),
            pltpu.VMEM((1, length), jnp.int32),
            pltpu.VMEM((length, features), jnp.bfloat16),
            pltpu.VMEM((length, heads * dk), jnp.bfloat16),
            pltpu.VMEM((length, heads * dv), jnp.bfloat16),
            pltpu.VMEM(weight.shape, jnp.bfloat16),
            pltpu.VMEM((count, rows, width), jnp.bfloat16),
            pltpu.VMEM((length, width), jnp.float32),
            pltpu.VMEM((heads, length, length), jnp.float32),
            pltpu.VMEM((128, length), jnp.float32),
            pltpu.VMEM((length, 128), jnp.float32),
            pltpu.VMEM((length, 128), jnp.float32),
            pltpu.VMEM((heads, dk, dv), jnp.float32),
            pltpu.VMEM((2 * heads, dk), jnp.float32),
            pltpu.VMEM((heads, dk, dv), jnp.bfloat16),
            pltpu.VMEM((2 * heads, dk), jnp.float32),
            pltpu.VMEM((heads, dk, dv), jnp.bfloat16),
            pltpu.VMEM((2 * heads, dk), jnp.float32),
            dma((7,)),
            dma((2,)), dma((Z, pieces)),
            dma((1,)), dma((Z, pieces)),
            dma((2,)), dma((2, Z, pieces)),
            dma((1,)), dma((2, Z, pieces, 2)),
            dma((heads + 1,)), dma((heads + 1,)),
        ],
        compiler_params=pltpu.CompilerParams(
            collective_id=0, has_side_effects=True, vmem_limit_bytes=60 * 1024 * 1024
        ),
        cost_estimate=pl.CostEstimate(
            flops=2 * length * features * width, bytes_accessed=6 * 1024 * 1024, transcendentals=0
        ),
    )(normed_input, weight, key_vectors, value_vectors, input_gate, forget_gate, resets)


def solution(mesh):
    sizes = mesh.shape
    return jax.shard_map(
        functools.partial(body, sizes["ctx"], sizes["dp"], sizes["groups"]),
        mesh=mesh,
        in_specs=(
            P(("groups", "dp"), "ctx", None),
            P(("dp", "ctx"), None),
            P(("groups", "dp"), "ctx", None),
            P(("groups", "dp"), "ctx", None),
            P(("groups", "dp"), None, "ctx"),
            P(("groups", "dp"), None, "ctx"),
            P(("groups", "dp"), "ctx"),
        ),
        out_specs=P(("groups", "dp"), "ctx", None),
        check_vma=False,
    )
```

```python
import functools

import jax
import jax.numpy as jnp
from jax import lax
from jax.experimental import pallas as pl
from jax.experimental.pallas import tpu as pltpu
from jax.sharding import PartitionSpec as P

very_low = -1e30
pieces, handed = 5, 3
lag_across, lag_over, lag_over_across = 2, 2, 4
MESH = pl.DeviceIdType.MESH


def dot(a, b, dims=((1,), (0,))):
    return lax.dot_general(a, b, (dims, ((), ())), preferred_element_type=jnp.float32)


def kernel(
    spread, Z, heads, x_hbm, w_hbm, k_hbm, v_hbm, ig_hbm, fg_hbm, rs_hbm, out_ref,
    gates, flags, xv, kv, vv, wown, wbuf, acc, prob, stack, cols, imax_scr, own_mem, own_info,
    mem_in, info_in, mem_out, info_out, q_out, q_in,
    lsem, zsend, zrecv, xsend, xrecv, ysend, yrecv, wsend, wrecv, msend, mrecv, qsend, qrecv, ssend, srecv,
):
    y = lax.axis_index("groups")
    d = lax.axis_index("dp")
    z = lax.axis_index("ctx")
    x, c = d // 2, d % 2
    up, down = (y, d, z + 1), (y, d, z - 1)
    across = (y, (1 - x) * 2 + c, z)
    over = (1 - y, d, z)
    mate = (y, x * 2 + 1 - c, z)
    length, features = kv.shape[0], xv.shape[1]
    dk = kv.shape[1] // heads
    dv = vv.shape[1] // heads
    factor = dk ** (-0.5)
    half = heads // 2
    rows = wbuf.shape[1] // 2
    high = rows // 4
    wide = wbuf.shape[2]

    def head_of(slot):
        return (slot + c * half) % heads

    def head_columns(slot, size):
        return pl.ds(pl.multiple_of(head_of(slot) * size, 128), size)

    local = [
        pltpu.make_async_copy(ig_hbm.at[0], gates.at[0, 0:heads], lsem.at[0]),
        pltpu.make_async_copy(fg_hbm.at[0], gates.at[1, 0:heads], lsem.at[1]),
        pltpu.make_async_copy(rs_hbm, flags, lsem.at[2]),
        pltpu.make_async_copy(x_hbm.at[0], xv.at[0:length], lsem.at[3]),
    ]
    if spread:
        fetch = pltpu.make_async_copy(
            w_hbm.at[:, pl.ds(pl.multiple_of(c * wide, 128), wide)],
            wbuf.at[x * Z + z, pl.ds(pl.multiple_of(c * rows, 16), rows), :],
            lsem.at[4],
        )
    else:
        fetch = pltpu.make_async_copy(w_hbm, wown, lsem.at[4])
    fetch.start()
    for h in range(heads):
        local.append(
            pltpu.make_async_copy(
                k_hbm.at[0, :, head_columns(h, dk)], kv.at[:, h * dk:(h + 1) * dk], lsem.at[5 + 2 * h]
            )
        )
        local.append(
            pltpu.make_async_copy(
                v_hbm.at[0, :, head_columns(h, dv)], vv.at[:, h * dv:(h + 1) * dv], lsem.at[6 + 2 * h]
            )
        )
    for one in local:
        one.start()

    barrier = pltpu.get_barrier_semaphore()

    def greet(device):
        pl.semaphore_signal(barrier, inc=1, device_id=device, device_id_type=MESH)

    @pl.when(z < Z - 1)
    def _():
        greet(up)

    @pl.when(z > 0)
    def _():
        greet(down)

    base = 0
    if spread:
        for device in (across, over, mate):
            greet(device)
        base = 3
    pl.semaphore_wait(
        barrier, base + jnp.where(z > 0, 1, 0) + jnp.where(z < Z - 1, 1, 0)
    )

    def mine(i):
        return jnp.where(i < handed, y * pieces + i, i)

    def theirs(i):
        return (1 - y) * pieces + i

    def piece(xx, zz, j):
        return wbuf.at[xx * Z + zz, pl.ds(pl.multiple_of(j * high, 16), high), :]

    def remote(src, dst, send, recv, device):
        return pltpu.make_async_remote_copy(
            src_ref=src, dst_ref=dst, send_sem=send, recv_sem=recv, device_id=device, device_id_type=MESH
        )

    def z_copy(way, zz, i):
        at = piece(x, zz, mine(i))
        return remote(at, at, zsend.at[way], zrecv.at[zz, i], up if way == 0 else down)

    def x_copy(xx, zz, i):
        at = piece(xx, zz, mine(i))
        return remote(at, at, xsend.at[0], xrecv.at[zz, i], across)

    def y_copy(xx, zz, i, j):
        at = piece(xx, zz, j)
        return remote(at, at, ysend.at[xx], yrecv.at[xx, zz, i], over)

    def w_copy(j):
        return remote(
            w_hbm.at[pl.ds(pl.multiple_of((j % 4) * high, 16), high), pl.ds(pl.multiple_of((1 - c) * wide, 128), wide)],
            piece(x, z, j), wsend.at[0], wrecv.at[j], mate,
        )

    def x_rows():
        return remote(x_hbm.at[0], xv.at[length:2 * length], msend.at[0], mrecv.at[0], mate)

    def q_copy(h):
        return remote(q_out.at[h], q_in.at[h], qsend.at[h], qrecv.at[h], mate)

    if spread:
        order = [mine(i) for i in range(pieces)] + [theirs(i) for i in range(handed)]
        for j in order:
            @pl.when(j // 4 == c)
            def _():
                w_copy(j).start()
        x_rows().start()
        fetch.wait()
        for from_mate in (0, 1):
            for i in range(pieces):
                @pl.when((mine(i) // 4 == c) == (from_mate == 0))
                def _():
                    if from_mate:
                        w_copy(mine(i)).wait_recv()

                    @pl.when(z < Z - 1)
                    def _():
                        z_copy(0, z, i).start()

                    @pl.when(z > 0)
                    def _():
                        z_copy(1, z, i).start()

                    x_copy(x, z, i).start()
        for i in range(handed):
            @pl.when(theirs(i) // 4 != c)
            def _():
                w_copy(theirs(i)).wait_recv()

    for one in local[:3]:
        one.wait()

    stack[...] = jnp.zeros_like(stack)
    for h in range(heads):
        f = gates[1, pl.ds(head_of(h), 1), :]
        stack[h:h + 1, :] = jnp.minimum(f, 0.0) - jnp.log1p(jnp.exp(-jnp.abs(f)))
        stack[8 + h:9 + h, :] = gates[0, pl.ds(head_of(h), 1), :]
    stack[4:5, :] = flags[...].astype(jnp.float32)
    run = stack[0:8, :]
    lane = lax.broadcasted_iota(jnp.int32, run.shape, 1)
    hop = 1
    while hop < length:
        run = run + jnp.where(lane >= hop, pltpu.roll(run, hop, 1), 0.0)
        hop *= 2
    stack[0:8, :] = run
    cols[...] = stack[...].T

    def row(at):
        return stack[at:at + 1, :]

    def col(at):
        return cols[:, at:at + 1]

    def last(at):
        return stack[at:at + 1, length - 1:length]

    def own_state(h):
        end_row = jnp.where(row(4) == last(4), last(h) - row(h) + row(8 + h), very_low)
        top = jnp.max(end_row, axis=1, keepdims=True)
        end_col = jnp.where(col(4) == last(4), last(h) - col(h) + col(8 + h), very_low)
        weighted = (
            kv[:, h * dk:(h + 1) * dk].astype(jnp.float32) * jnp.exp(end_col - top)
        ).astype(jnp.bfloat16)
        own_mem[h] = dot(weighted, vv[:, h * dv:(h + 1) * dv], ((0,), (0,)))
        own_info[h:h + 1, :] = jnp.sum(weighted.astype(jnp.float32), axis=0, keepdims=True)
        own_info[heads + h:heads + h + 1, :] = jnp.broadcast_to(top, (1, dk))

    def decay(h):
        row_at = lax.broadcasted_iota(jnp.int32, (length, length), 0)
        col_at = lax.broadcasted_iota(jnp.int32, (length, length), 1)
        linked = jnp.logical_and(col(4) == row(4), row_at >= col_at)
        exponent = jnp.where(linked, col(h) - row(h) + row(8 + h), very_low)
        top = jnp.max(exponent, axis=1, keepdims=True)
        imax_scr[:, h:h + 1] = top
        prob[h] = jnp.exp(exponent - top) * factor

    def info_copy():
        return pltpu.make_async_remote_copy(
            src_ref=info_out, dst_ref=info_in, send_sem=ssend.at[heads], recv_sem=srecv.at[heads],
            device_id=up, device_id_type=MESH,
        )

    def mem_copy(h):
        return pltpu.make_async_remote_copy(
            src_ref=mem_out.at[h], dst_ref=mem_in.at[h], send_sem=ssend.at[h], recv_sem=srecv.at[h],
            device_id=up, device_id_type=MESH,
        )

    def pass_head(h):
        if h == 0:
            @pl.when(z > 0)
            def _():
                info_copy().wait_recv()

        @pl.when(z > 0)
        def _():
            mem_copy(h).wait_recv()

        @pl.when(z < Z - 1)
        def _():
            def blend(at):
                gap = jnp.where(last(4) > 0, very_low, last(at))
                shifted = info_in[heads + at:heads + at + 1, :] + gap
                top = own_info[heads + at:heads + at + 1, :]
                both = jnp.maximum(shifted, top)
                return both, jnp.exp(shifted - both), jnp.exp(top - both)

            if h == 0:
                for at in range(heads):
                    both, early, late = blend(at)
                    info_out[at:at + 1, :] = early * info_in[at:at + 1, :] + late * own_info[at:at + 1, :]
                    info_out[heads + at:heads + at + 1, :] = both
                info_copy().start()
            _, early, late = blend(h)
            mem_out[h] = (
                early[:, 0:1] * mem_in[h].astype(jnp.float32) + late[:, 0:1] * own_mem[h]
            ).astype(jnp.bfloat16)
            mem_copy(h).start()

    def start_state():
        for one in local[4:]:
            one.wait()
        for h in range(heads):
            own_state(h)

        @pl.when(z == 0)
        def _():
            mem_in[...] = jnp.zeros_like(mem_in)
            info_in[0:heads, :] = jnp.zeros((heads, dk), jnp.float32)
            info_in[heads:, :] = jnp.full((heads, dk), very_low, jnp.float32)
            for h in range(heads):
                pass_head(h)

    if not spread:
        start_state()

        @pl.when(z > 0)
        def _():
            for h in range(heads):
                pass_head(h)

        for h in range(heads):
            decay(h)
        local[3].wait()
        fetch.wait()

    if spread:
        state_steps = [-(-2 * pieces * (h + 1) // 5) for h in range(heads)]
        catch_up = (Z - 1) * pieces

        def multiply(xx, zz, side):
            here = slice(side * length, (side + 1) * length)
            for cc in (0, 1):
                at = pl.ds(pl.multiple_of(((xx * 2 + cc) * Z + zz) * rows, 128), rows)
                acc[here, :] += dot(xv[here, at], wbuf[xx * Z + zz, cc * rows:(cc + 1) * rows, :])

        def places(s, low):
            q = (s + 2 * pieces) // pieces - 2
            p = (s + 2 * pieces) % pieces
            below, above = z - q, z + q
            yield below, p, jnp.logical_and(q >= low, jnp.logical_and(q < Z, below >= 0))
            yield above, p, jnp.logical_and(q >= max(low, 1), above < Z)

        def take(t, side):
            for xx, lag, low in ((x, lag_over, 1), (1 - x, lag_over_across, 0)):
                for zz, i, ok in places(t - lag, low):
                    @pl.when(jnp.logical_and(ok, i == pieces - 1))
                    def _():
                        multiply(xx, zz, side)

        def one_step(t, carry):
            for way, (zz, i, ok) in enumerate(places(t, 1)):
                @pl.when(ok)
                def _():
                    z_copy(way, zz, i).wait_recv()

                    @pl.when(z < Z - 1 if way == 0 else z > 0)
                    def _():
                        z_copy(way, zz, i).start()

                    x_copy(x, zz, i).start()

                    @pl.when(i < handed)
                    def _():
                        y_copy(x, zz, i, mine(i)).start()

            for zz, i, ok in places(t - lag_across, 0):
                @pl.when(ok)
                def _():
                    x_copy(1 - x, zz, i).wait_recv()

                    @pl.when(i < handed)
                    def _():
                        y_copy(1 - x, zz, i, mine(i)).start()

            for h in range(heads):
                @pl.when(jnp.logical_and(t == z * pieces + state_steps[h], jnp.logical_and(z > 0, z < Z - 1)))
                def _():
                    pass_head(h)

            @pl.when(t == lag_across + 1)
            def _():
                start_state()
                local[3].wait()
                acc[...] = jnp.zeros_like(acc)
                multiply(x, z, 0)

            for h in range(heads):
                @pl.when(t == pieces + 1 + h * (pieces // 2))
                def _():
                    decay(h)

            for xx, lag, low in ((x, lag_over, 1), (1 - x, lag_over_across, 0)):
                for zz, i, ok in places(t - lag, low):
                    @pl.when(jnp.logical_and(ok, i < handed))
                    def _():
                        y_copy(xx, zz, i, theirs(i)).wait_recv()

            take(t, 0)

            @pl.when(t == catch_up)
            def _():
                x_rows().wait_recv()
                multiply(x, z, 1)

                def earlier(before, carry):
                    take(before, 1)
                    return carry

                lax.fori_loop(1, catch_up, earlier, 0)

            @pl.when(t >= catch_up)
            def _():
                take(t, 1)

            return carry

        lax.fori_loop(1, Z * pieces + lag_over_across, one_step, 0)

        for h in range(half):
            q_out[h] = acc[length:2 * length, h * dk:(h + 1) * dk].astype(jnp.bfloat16)
            q_copy(h).start()

        @pl.when(z == Z - 1)
        def _():
            for h in range(heads):
                pass_head(h)

    else:
        acc[...] = jnp.zeros_like(acc)

        def one_block(at, carry):
            here = pl.ds(pl.multiple_of(at * 256, 256), 256)
            acc[...] += dot(xv[:, here], wown[here, :])
            return carry

        lax.fori_loop(0, features // 256, one_block, 0)

    info = info_in[...]
    for h in range(heads):
        if not spread:
            q = acc[:, head_columns(h, dk)].astype(jnp.bfloat16)
        elif h < half:
            q = acc[0:length, h * dk:(h + 1) * dk].astype(jnp.bfloat16)
        else:
            q_copy(h - half).wait_recv()
            q = q_in[h - half]
        values = vv[:, h * dv:(h + 1) * dv]
        scores = dot(q, kv[:, h * dk:(h + 1) * dk], ((1,), (1,)))
        weighted = (scores * prob[h]).astype(jnp.bfloat16)
        inner = dot(weighted, values)
        inner_den = jnp.sum(weighted.astype(jnp.float32), axis=1, keepdims=True)
        cross = dot(q, mem_in[h])
        normer = info[h:h + 1, :].astype(jnp.bfloat16).astype(jnp.float32)
        cross_den = jnp.sum(q.astype(jnp.float32) * normer, axis=1, keepdims=True)
        top = imax_scr[:, h:h + 1]
        carried = jnp.where(col(4) == 0, col(h) + info[heads + h:heads + h + 1, 0:1], very_low)
        row_max = jnp.maximum(top, carried)
        a = jnp.exp(top - row_max)
        b = jnp.exp(carried - row_max) * factor
        den = a * inner_den + b * cross_den
        inverse = 1.0 / jnp.maximum(jnp.abs(den), jnp.exp(jnp.maximum(-row_max, 0.0)))
        hidden = (a * inverse) * inner + (b * inverse) * cross
        out_ref[0, :, head_columns(h, dv)] = hidden.astype(jnp.bfloat16)

    @pl.when(z < Z - 1)
    def _():
        info_copy().wait_send()
        for h in range(heads):
            mem_copy(h).wait_send()

    if spread:
        def drain(sem, count, tall):
            some = wbuf.at[0:count, 0:tall, :]
            remote(some, some, sem, sem, mate).wait_send()

        for at in range(Z):
            @pl.when(z == at)
            def _():
                if at < Z - 1:
                    drain(zsend.at[0], at + 1, pieces * high)
                if at > 0:
                    drain(zsend.at[1], Z - at, pieces * high)

        drain(xsend.at[0], Z, pieces * high)
        drain(ysend.at[x], Z - 1, handed * high)
        drain(ysend.at[1 - x], Z, handed * high)
        drain(wsend.at[0], 1, rows)
        x_rows().wait_send()
        for h in range(half):
            q_copy(h).wait_send()


def body(Z, dp, planes, normed_input, query_weight, key_vectors, value_vectors, input_gate, forget_gate, resets):
    _, length, features = normed_input.shape
    heads = input_gate.shape[1]
    width = query_weight.shape[1]
    dk = key_vectors.shape[2] // heads
    dv = value_vectors.shape[2] // heads
    spread = dp == 4 and planes == 2 and query_weight.shape[0] % 256 == 0
    if spread:
        rows = query_weight.shape[0]
        weight = query_weight
    else:
        rows = 64
        weight = lax.all_gather(query_weight, ("dp", "ctx"), axis=0, tiled=True)
    count = features // (2 * rows) if spread else 1
    dma = pltpu.SemaphoreType.DMA
    hbm = pl.BlockSpec(memory_space=pltpu.HBM)
    vmem = pl.BlockSpec(memory_space=pltpu.VMEM)
    return pl.pallas_call(
        functools.partial(kernel, spread, Z, heads),
        out_shape=jax.ShapeDtypeStruct((1, length, heads * dv), jnp.bfloat16),
        in_specs=[hbm] * 7,
        out_specs=vmem,
        scratch_shapes=[
            pltpu.VMEM((2, 8, length), jnp.float32),
            pltpu.VMEM((1, length), jnp.int32),
            pltpu.VMEM((2 * length if spread else length, features), jnp.bfloat16),
            pltpu.VMEM((length, heads * dk), jnp.bfloat16),
            pltpu.VMEM((length, heads * dv), jnp.bfloat16),
            pltpu.VMEM((16, 128) if spread else weight.shape, jnp.bfloat16),
            pltpu.VMEM((count, 2 * rows, width // 2), jnp.bfloat16),
            pltpu.VMEM((2 * length, width // 2) if spread else (length, width), jnp.float32),
            pltpu.VMEM((heads, length, length), jnp.float32),
            pltpu.VMEM((128, length), jnp.float32),
            pltpu.VMEM((length, 128), jnp.float32),
            pltpu.VMEM((length, 128), jnp.float32),
            pltpu.VMEM((heads, dk, dv), jnp.float32),
            pltpu.VMEM((2 * heads, dk), jnp.float32),
            pltpu.VMEM((heads, dk, dv), jnp.bfloat16),
            pltpu.VMEM((2 * heads, dk), jnp.float32),
            pltpu.VMEM((heads, dk, dv), jnp.bfloat16),
            pltpu.VMEM((2 * heads, dk), jnp.float32),
            pltpu.VMEM((heads // 2, length, dk), jnp.bfloat16),
            pltpu.VMEM((heads // 2, length, dk), jnp.bfloat16),
            dma((5 + 2 * heads,)),
            dma((2,)), dma((Z, pieces)),
            dma((1,)), dma((Z, pieces)),
            dma((2,)), dma((2, Z, handed)),
            dma((1,)), dma((8,)),
            dma((1,)), dma((1,)),
            dma((heads // 2,)), dma((heads // 2,)),
            dma((heads + 1,)), dma((heads + 1,)),
        ],
        compiler_params=pltpu.CompilerParams(
            collective_id=0, has_side_effects=True, vmem_limit_bytes=60 * 1024 * 1024
        ),
        cost_estimate=pl.CostEstimate(
            flops=2 * length * features * width, bytes_accessed=6 * 1024 * 1024, transcendentals=0
        ),
    )(normed_input, weight, key_vectors, value_vectors, input_gate, forget_gate, resets)


def solution(mesh):
    sizes = mesh.shape
    return jax.shard_map(
        functools.partial(body, sizes["ctx"], sizes["dp"], sizes["groups"]),
        mesh=mesh,
        in_specs=(
            P(("groups", "dp"), "ctx", None),
            P(("dp", "ctx"), None),
            P(("groups", "dp"), "ctx", None),
            P(("groups", "dp"), "ctx", None),
            P(("groups", "dp"), None, "ctx"),
            P(("groups", "dp"), None, "ctx"),
            P(("groups", "dp"), "ctx"),
        ),
        out_specs=P(("groups", "dp"), "ctx", None),
        check_vma=False,
    )
```

```python
import functools

import jax
import jax.numpy as jnp
from jax import lax
from jax.experimental import pallas as pl
from jax.experimental.pallas import tpu as pltpu
from jax.sharding import PartitionSpec as P

very_low = -1e30
shared_columns = 384
pieces = 4
lag_across, lag_over, lag_over_across, lag_mate, lag_mate_across = 2, 2, 4, 5, 7
MESH = pl.DeviceIdType.MESH


def dot(a, b, dims=((1,), (0,))):
    return lax.dot_general(a, b, (dims, ((), ())), preferred_element_type=jnp.float32)


def kernel(
    spread, Z, heads, x_hbm, w_hbm, k_hbm, v_hbm, ig_hbm, fg_hbm, rs_hbm, out_ref,
    gates, flags, xv, kv, vv, wown, wbuf, acc, prob, stack, cols, imax_scr, own_mem, own_info,
    mem_in, info_in, mem_out, info_out,
    lsem, zsend, zrecv, xsend, xrecv, ysend, yrecv, csend, crecv, ssend, srecv,
):
    y = lax.axis_index("groups")
    d = lax.axis_index("dp")
    z = lax.axis_index("ctx")
    x, c = d // 2, d % 2
    up, down = (y, d, z + 1), (y, d, z - 1)
    across = (y, (1 - x) * 2 + c, z)
    over = (1 - y, d, z)
    mate = (y, x * 2 + 1 - c, z)
    length, features = xv.shape
    dk = kv.shape[1] // heads
    dv = vv.shape[1] // heads
    factor = dk ** (-0.5)
    width = acc.shape[1]
    rows = wbuf.shape[1]
    A = shared_columns

    local = [
        pltpu.make_async_copy(ig_hbm.at[0], gates.at[0, 0:heads], lsem.at[4]),
        pltpu.make_async_copy(fg_hbm.at[0], gates.at[1, 0:heads], lsem.at[5]),
        pltpu.make_async_copy(rs_hbm, flags, lsem.at[6]),
        pltpu.make_async_copy(k_hbm.at[0], kv, lsem.at[0]),
        pltpu.make_async_copy(v_hbm.at[0], vv, lsem.at[1]),
        pltpu.make_async_copy(x_hbm.at[0], xv, lsem.at[2]),
        pltpu.make_async_copy(w_hbm, wown, lsem.at[3]),
    ]
    for one in local:
        one.start()

    barrier = pltpu.get_barrier_semaphore()

    def greet(device):
        pl.semaphore_signal(barrier, inc=1, device_id=device, device_id_type=MESH)

    @pl.when(z < Z - 1)
    def _():
        greet(up)

    @pl.when(z > 0)
    def _():
        greet(down)

    base = 0
    if spread:
        for device in (across, over, mate):
            greet(device)
        base = 3
    pl.semaphore_wait(
        barrier, base + jnp.where(z > 0, 1, 0) + jnp.where(z < Z - 1, 1, 0)
    )

    B = width - 2 * A

    def columns(part):
        if part == 0:
            return pl.ds(pl.multiple_of(y * A, 128), A + B)
        if part == 1:
            return pl.ds(pl.multiple_of(y * (A + B), 128), A)
        return pl.ds(pl.multiple_of((1 - y) * (A + B), 128), A)

    high = rows // pieces

    def shard(xx, cc, zz):
        return (xx * 2 + cc) * Z + zz

    def remote(xx, cc, zz, p, part, send, recv, device, own=False):
        at = pl.ds(p * high if isinstance(p, int) else pl.multiple_of(p * high, 16), high)
        there = wbuf.at[shard(xx, cc, zz), at, columns(part)]
        here = w_hbm.at[at, columns(part)] if own else there
        return pltpu.make_async_remote_copy(
            src_ref=here, dst_ref=there, send_sem=send, recv_sem=recv,
            device_id=device, device_id_type=MESH,
        )

    def z_copy(way, zz, p, own=False):
        device = up if way == 0 else down
        return remote(x, c, zz, p, 0, zsend.at[way], zrecv.at[zz, p], device, own)

    def x_copy(xx, zz, p, own=False):
        return remote(xx, c, zz, p, 0, xsend.at[0], xrecv.at[zz, p], across, own)

    def y_copy(xx, zz, p, part):
        return remote(xx, c, zz, p, part, ysend.at[xx], yrecv.at[xx, zz, p], over)

    def c_copy(xx, cc, zz, p, part, own=False):
        return remote(
            xx, cc, zz, p, part, csend.at[0], crecv.at[xx, zz, p, part // 2], mate, own
        )

    if spread:
        for p in range(pieces):
            @pl.when(z < Z - 1)
            def _():
                z_copy(0, z, p, True).start()

            @pl.when(z > 0)
            def _():
                z_copy(1, z, p, True).start()

            x_copy(x, z, p, True).start()
        for p in range(pieces):
            for part in (0, 2):
                c_copy(x, c, z, p, part, True).start()

    for one in local[:3]:
        one.wait()

    f = gates[1, 0:heads, :]
    stack[...] = jnp.zeros_like(stack)
    stack[0:heads, :] = jnp.minimum(f, 0.0) - jnp.log1p(jnp.exp(-jnp.abs(f)))
    stack[4:5, :] = flags[...].astype(jnp.float32)
    run = stack[0:8, :]
    lane = lax.broadcasted_iota(jnp.int32, run.shape, 1)
    hop = 1
    while hop < length:
        run = run + jnp.where(lane >= hop, pltpu.roll(run, hop, 1), 0.0)
        hop *= 2
    stack[0:8, :] = run
    stack[8:8 + heads, :] = gates[0, 0:heads, :]
    cols[...] = stack[...].T

    def row(at):
        return stack[at:at + 1, :]

    def col(at):
        return cols[:, at:at + 1]

    def last(at):
        return stack[at:at + 1, length - 1:length]

    def own_state(h):
        end_row = jnp.where(row(4) == last(4), last(h) - row(h) + row(8 + h), very_low)
        top = jnp.max(end_row, axis=1, keepdims=True)
        end_col = jnp.where(col(4) == last(4), last(h) - col(h) + col(8 + h), very_low)
        weighted = (
            kv[:, h * dk:(h + 1) * dk].astype(jnp.float32) * jnp.exp(end_col - top)
        ).astype(jnp.bfloat16)
        own_mem[h] = dot(weighted, vv[:, h * dv:(h + 1) * dv], ((0,), (0,)))
        own_info[h:h + 1, :] = jnp.sum(weighted.astype(jnp.float32), axis=0, keepdims=True)
        own_info[heads + h:heads + h + 1, :] = jnp.broadcast_to(top, (1, dk))

    def decay(h):
        row_at = lax.broadcasted_iota(jnp.int32, (length, length), 0)
        col_at = lax.broadcasted_iota(jnp.int32, (length, length), 1)
        linked = jnp.logical_and(col(4) == row(4), row_at >= col_at)
        exponent = jnp.where(linked, col(h) - row(h) + row(8 + h), very_low)
        top = jnp.max(exponent, axis=1, keepdims=True)
        imax_scr[:, h:h + 1] = top
        prob[h] = jnp.exp(exponent - top) * factor

    def info_copy():
        return pltpu.make_async_remote_copy(
            src_ref=info_out, dst_ref=info_in, send_sem=ssend.at[heads], recv_sem=srecv.at[heads],
            device_id=up, device_id_type=MESH,
        )

    def mem_copy(h):
        return pltpu.make_async_remote_copy(
            src_ref=mem_out.at[h], dst_ref=mem_in.at[h], send_sem=ssend.at[h], recv_sem=srecv.at[h],
            device_id=up, device_id_type=MESH,
        )

    def pass_head(h):
        if h == 0:
            @pl.when(z > 0)
            def _():
                info_copy().wait_recv()

        @pl.when(z > 0)
        def _():
            mem_copy(h).wait_recv()

        @pl.when(z < Z - 1)
        def _():
            def blend(at):
                gap = jnp.where(last(4) > 0, very_low, last(at))
                shifted = info_in[heads + at:heads + at + 1, :] + gap
                top = own_info[heads + at:heads + at + 1, :]
                both = jnp.maximum(shifted, top)
                return both, jnp.exp(shifted - both), jnp.exp(top - both)

            if h == 0:
                for at in range(heads):
                    both, early, late = blend(at)
                    info_out[at:at + 1, :] = early * info_in[at:at + 1, :] + late * own_info[at:at + 1, :]
                    info_out[heads + at:heads + at + 1, :] = both
                info_copy().start()
            _, early, late = blend(h)
            mem_out[h] = (
                early[:, 0:1] * mem_in[h].astype(jnp.float32) + late[:, 0:1] * own_mem[h]
            ).astype(jnp.bfloat16)
            mem_copy(h).start()

    def start_state():
        for one in local[3:5]:
            one.wait()
        for h in range(heads):
            own_state(h)
        hand_on_first()

    def hand_on_first():
        @pl.when(z == 0)
        def _():
            mem_in[...] = jnp.zeros_like(mem_in)
            info_in[0:heads, :] = jnp.zeros((heads, dk), jnp.float32)
            info_in[heads:, :] = jnp.full((heads, dk), very_low, jnp.float32)
            for h in range(heads):
                pass_head(h)

    if not spread:
        start_state()

        @pl.when(z > 0)
        def _():
            for h in range(heads):
                pass_head(h)

        for h in range(heads):
            decay(h)
        for one in local[5:]:
            one.wait()

    def multiply(at, piece):
        part = xv[:, pl.ds(pl.multiple_of(at * rows, 128), rows)]
        acc[...] += dot(part, piece)

    if spread:
        state_steps = [3 - (-2 * pieces * (h + 1) // 5) for h in range(heads)]
        def places(s, low):
            q = (s + 2 * pieces) // pieces - 2
            p = (s + 2 * pieces) % pieces
            below, above = z - q, z + q
            yield below, p, jnp.logical_and(q >= low, jnp.logical_and(q < Z, below >= 0))
            yield above, p, jnp.logical_and(q >= max(low, 1), above < Z)

        def take(xx, cc, zz, p):
            @pl.when(p == pieces - 1)
            def _():
                multiply(shard(xx, cc, zz), wbuf[shard(xx, cc, zz)])

        def one_step(t, carry):
            for way, (zz, p, ok) in enumerate(places(t, 1)):
                @pl.when(ok)
                def _():
                    z_copy(way, zz, p).wait_recv()

                    @pl.when(z < Z - 1 if way == 0 else z > 0)
                    def _():
                        z_copy(way, zz, p).start()

                    x_copy(x, zz, p).start()
                    y_copy(x, zz, p, 1).start()
                    c_copy(x, c, zz, p, 0).start()

            for zz, p, ok in places(t - lag_across, 0):
                @pl.when(ok)
                def _():
                    x_copy(1 - x, zz, p).wait_recv()
                    y_copy(1 - x, zz, p, 1).start()
                    c_copy(1 - x, c, zz, p, 0).start()

            for h in range(heads):
                @pl.when(t == pieces + h)
                def _():
                    if h == 0:
                        for one in local[3:5]:
                            one.wait()
                    own_state(h)

            @pl.when(t == pieces + heads)
            def _():
                hand_on_first()

            for h in range(heads):
                @pl.when(jnp.logical_and(t == z * pieces + state_steps[h], jnp.logical_and(z > 0, z < Z - 1)))
                def _():
                    pass_head(h)

            @pl.when(t == pieces + 1)
            def _():
                for one in local[5:]:
                    one.wait()
                acc[...] = dot(
                    xv[:, pl.ds(pl.multiple_of(shard(x, c, z) * rows, 128), rows)], wown[...]
                )

            for h in range(heads):
                @pl.when(t == 2 * pieces + h * (pieces // 2))
                def _():
                    decay(h)

            for zz, p, ok in places(t - lag_over, 1):
                @pl.when(ok)
                def _():
                    y_copy(x, zz, p, 2).wait_recv()
                    c_copy(x, c, zz, p, 2).start()
                    take(x, c, zz, p)

            for zz, p, ok in places(t - lag_over_across, 0):
                @pl.when(ok)
                def _():
                    y_copy(1 - x, zz, p, 2).wait_recv()
                    c_copy(1 - x, c, zz, p, 2).start()
                    take(1 - x, c, zz, p)

            for zz, p, ok in places(t - lag_mate, 0):
                @pl.when(ok)
                def _():
                    for part in (0, 2):
                        c_copy(x, 1 - c, zz, p, part).wait_recv()
                    take(x, 1 - c, zz, p)

            for zz, p, ok in places(t - lag_mate_across, 0):
                @pl.when(ok)
                def _():
                    for part in (0, 2):
                        c_copy(1 - x, 1 - c, zz, p, part).wait_recv()
                    take(1 - x, 1 - c, zz, p)

            return carry

        lax.fori_loop(1, Z * pieces + lag_mate_across, one_step, 0)

        @pl.when(z == Z - 1)
        def _():
            for h in range(heads):
                pass_head(h)

    else:
        acc[...] = jnp.zeros_like(acc)

        def one_block(at, carry):
            multiply(at, wown[pl.ds(pl.multiple_of(at * rows, 16), rows), :])
            return carry

        lax.fori_loop(0, features // rows, one_block, 0)

    info = info_in[...]
    for h in range(heads):
        q = acc[:, h * dk:(h + 1) * dk].astype(jnp.bfloat16)
        values = vv[:, h * dv:(h + 1) * dv]
        scores = dot(q, kv[:, h * dk:(h + 1) * dk], ((1,), (1,)))
        weighted = (scores * prob[h]).astype(jnp.bfloat16)
        inner = dot(weighted, values)
        inner_den = jnp.sum(weighted.astype(jnp.float32), axis=1, keepdims=True)
        cross = dot(q, mem_in[h])
        normer = info[h:h + 1, :].astype(jnp.bfloat16).astype(jnp.float32)
        cross_den = jnp.sum(q.astype(jnp.float32) * normer, axis=1, keepdims=True)
        top = imax_scr[:, h:h + 1]
        carried = jnp.where(col(4) == 0, col(h) + info[heads + h:heads + h + 1, 0:1], very_low)
        row_max = jnp.maximum(top, carried)
        a = jnp.exp(top - row_max)
        b = jnp.exp(carried - row_max) * factor
        den = a * inner_den + b * cross_den
        inverse = 1.0 / jnp.maximum(jnp.abs(den), jnp.exp(jnp.maximum(-row_max, 0.0)))
        hidden = (a * inverse) * inner + (b * inverse) * cross
        out_ref[0, :, h * dv:(h + 1) * dv] = hidden.astype(jnp.bfloat16)

    @pl.when(z < Z - 1)
    def _():
        info_copy().wait_send()
        for h in range(heads):
            mem_copy(h).wait_send()

    if spread:
        def drain(sem, count, wide):
            some = wbuf.at[0:count, :, 0:wide]
            pltpu.make_async_remote_copy(
                src_ref=some, dst_ref=some, send_sem=sem, recv_sem=sem, device_id=mate, device_id_type=MESH
            ).wait_send()

        for at in range(Z):
            @pl.when(z == at)
            def _():
                if at < Z - 1:
                    drain(zsend.at[0], at + 1, A + B)
                if at > 0:
                    drain(zsend.at[1], Z - at, A + B)

        drain(xsend.at[0], Z, A + B)
        drain(ysend.at[x], Z - 1, A)
        drain(ysend.at[1 - x], Z, A)
        drain(csend.at[0], 2 * Z, width)


def body(Z, dp, planes, normed_input, query_weight, key_vectors, value_vectors, input_gate, forget_gate, resets):
    _, length, features = normed_input.shape
    heads = input_gate.shape[1]
    width = query_weight.shape[1]
    dk = key_vectors.shape[2] // heads
    dv = value_vectors.shape[2] // heads
    spread = dp == 4 and planes == 2 and query_weight.shape[0] % 256 == 0
    if spread:
        rows = query_weight.shape[0]
        weight = query_weight
    else:
        rows = 256
        weight = lax.all_gather(query_weight, ("dp", "ctx"), axis=0, tiled=True)
    count = features // rows if spread else 1
    dma = pltpu.SemaphoreType.DMA
    hbm = pl.BlockSpec(memory_space=pltpu.HBM)
    vmem = pl.BlockSpec(memory_space=pltpu.VMEM)
    return pl.pallas_call(
        functools.partial(kernel, spread, Z, heads),
        out_shape=jax.ShapeDtypeStruct((1, length, heads * dv), jnp.bfloat16),
        in_specs=[hbm] * 7,
        out_specs=vmem,
        scratch_shapes=[
            pltpu.VMEM((2, 8, length), jnp.float32),
            pltpu.VMEM((1, length), jnp.int32),
            pltpu.VMEM((length, features), jnp.bfloat16),
            pltpu.VMEM((length, heads * dk), jnp.bfloat16),
            pltpu.VMEM((length, heads * dv), jnp.bfloat16),
            pltpu.VMEM(weight.shape, jnp.bfloat16),
            pltpu.VMEM((count, rows, width), jnp.bfloat16),
            pltpu.VMEM((length, width), jnp.float32),
            pltpu.VMEM((heads, length, length), jnp.float32),
            pltpu.VMEM((128, length), jnp.float32),
            pltpu.VMEM((length, 128), jnp.float32),
            pltpu.VMEM((length, 128), jnp.float32),
            pltpu.VMEM((heads, dk, dv), jnp.float32),
            pltpu.VMEM((2 * heads, dk), jnp.float32),
            pltpu.VMEM((heads, dk, dv), jnp.bfloat16),
            pltpu.VMEM((2 * heads, dk), jnp.float32),
            pltpu.VMEM((heads, dk, dv), jnp.bfloat16),
            pltpu.VMEM((2 * heads, dk), jnp.float32),
            dma((7,)),
            dma((2,)), dma((Z, pieces)),
            dma((1,)), dma((Z, pieces)),
            dma((2,)), dma((2, Z, pieces)),
            dma((1,)), dma((2, Z, pieces, 2)),
            dma((heads + 1,)), dma((heads + 1,)),
        ],
        compiler_params=pltpu.CompilerParams(
            collective_id=0, has_side_effects=True, vmem_limit_bytes=60 * 1024 * 1024
        ),
        cost_estimate=pl.CostEstimate(
            flops=2 * length * features * width, bytes_accessed=6 * 1024 * 1024, transcendentals=0
        ),
    )(normed_input, weight, key_vectors, value_vectors, input_gate, forget_gate, resets)


def solution(mesh):
    sizes = mesh.shape
    return jax.shard_map(
        functools.partial(body, sizes["ctx"], sizes["dp"], sizes["groups"]),
        mesh=mesh,
        in_specs=(
            P(("groups", "dp"), "ctx", None),
            P(("dp", "ctx"), None),
            P(("groups", "dp"), "ctx", None),
            P(("groups", "dp"), "ctx", None),
            P(("groups", "dp"), None, "ctx"),
            P(("groups", "dp"), None, "ctx"),
            P(("groups", "dp"), "ctx"),
        ),
        out_specs=P(("groups", "dp"), "ctx", None),
        check_vma=False,
    )
```

```python
import functools

import jax
import jax.numpy as jnp
from jax import lax
from jax.experimental import pallas as pl
from jax.experimental.pallas import tpu as pltpu
from jax.sharding import PartitionSpec as P

very_low = -1e30
shared_columns = 384
pieces = 4
early = 2
lag_across, lag_over, lag_over_across, lag_mate, lag_mate_across = 2, 2, 4, 5, 7
MESH = pl.DeviceIdType.MESH


def dot(a, b, dims=((1,), (0,))):
    return lax.dot_general(a, b, (dims, ((), ())), preferred_element_type=jnp.float32)


def kernel(
    spread, Z, heads, x_hbm, w_hbm, k_hbm, v_hbm, ig_hbm, fg_hbm, rs_hbm, out_ref,
    gates, flags, xv, kv, vv, wown, wbuf, acc, prob, stack, cols, imax_scr, own_mem, own_info,
    mem_in, info_in, mem_out, info_out,
    lsem, zsend, zrecv, xsend, xrecv, esend, erecv, ysend, yrecv, csend, crecv, ssend, srecv,
):
    y = lax.axis_index("groups")
    d = lax.axis_index("dp")
    z = lax.axis_index("ctx")
    x, c = d // 2, d % 2
    up, down = (y, d, z + 1), (y, d, z - 1)
    across = (y, (1 - x) * 2 + c, z)
    over = (1 - y, d, z)
    mate = (y, x * 2 + 1 - c, z)
    length, features = xv.shape
    dk = kv.shape[1] // heads
    dv = vv.shape[1] // heads
    factor = dk ** (-0.5)
    width = acc.shape[1]
    rows = wbuf.shape[1]
    A = shared_columns

    local = [
        pltpu.make_async_copy(ig_hbm.at[0], gates.at[0, 0:heads], lsem.at[4]),
        pltpu.make_async_copy(fg_hbm.at[0], gates.at[1, 0:heads], lsem.at[5]),
        pltpu.make_async_copy(rs_hbm, flags, lsem.at[6]),
        pltpu.make_async_copy(k_hbm.at[0], kv, lsem.at[0]),
        pltpu.make_async_copy(v_hbm.at[0], vv, lsem.at[1]),
        pltpu.make_async_copy(x_hbm.at[0], xv, lsem.at[2]),
        pltpu.make_async_copy(w_hbm, wown, lsem.at[3]),
    ]
    for one in local:
        one.start()

    barrier = pltpu.get_barrier_semaphore()

    def greet(device):
        pl.semaphore_signal(barrier, inc=1, device_id=device, device_id_type=MESH)

    @pl.when(z < Z - 1)
    def _():
        greet(up)

    @pl.when(z > 0)
    def _():
        greet(down)

    base = 0
    if spread:
        for device in (across, over, mate):
            greet(device)
        base = 3
    pl.semaphore_wait(
        barrier, base + jnp.where(z > 0, 1, 0) + jnp.where(z < Z - 1, 1, 0)
    )

    B = width - 2 * A

    def columns(part):
        if part == 0:
            return pl.ds(pl.multiple_of(y * A, 128), A + B)
        if part == 1:
            return pl.ds(pl.multiple_of(y * (A + B), 128), A)
        return pl.ds(pl.multiple_of((1 - y) * (A + B), 128), A)

    high = rows // pieces

    def shard(xx, cc, zz):
        return (xx * 2 + cc) * Z + zz

    def remote(xx, cc, zz, p, part, send, recv, device, own=False):
        at = pl.ds(p * high if isinstance(p, int) else pl.multiple_of(p * high, 16), high)
        there = wbuf.at[shard(xx, cc, zz), at, columns(part)]
        here = w_hbm.at[at, columns(part)] if own else there
        return pltpu.make_async_remote_copy(
            src_ref=here, dst_ref=there, send_sem=send, recv_sem=recv,
            device_id=device, device_id_type=MESH,
        )

    def z_copy(way, zz, p, own=False):
        device = up if way == 0 else down
        return remote(x, c, zz, p, 0, zsend.at[way], zrecv.at[zz, p], device, own)

    def x_copy(xx, zz, p, own=False):
        return remote(xx, c, zz, p, 0, xsend.at[0], xrecv.at[zz, p], across, own)

    def e_copy(xx, p, own=False):
        return remote(xx, c, z, p, 2, esend.at[0], erecv.at[p], across, own)

    def y_copy(xx, zz, p, part):
        return remote(xx, c, zz, p, part, ysend.at[xx], yrecv.at[xx, zz, p], over)

    def c_copy(xx, cc, zz, p, part, own=False):
        return remote(
            xx, cc, zz, p, part, csend.at[0], crecv.at[xx, zz, p, part // 2], mate, own
        )

    if spread:
        for p in range(pieces):
            @pl.when(z < Z - 1)
            def _():
                z_copy(0, z, p, True).start()

            @pl.when(z > 0)
            def _():
                z_copy(1, z, p, True).start()

            x_copy(x, z, p, True).start()
            if p >= pieces - early:
                e_copy(x, p, True).start()
        for p in range(pieces):
            for part in (0, 2):
                c_copy(x, c, z, p, part, True).start()

    for one in local[:3]:
        one.wait()

    f = gates[1, 0:heads, :]
    stack[...] = jnp.zeros_like(stack)
    stack[0:heads, :] = jnp.minimum(f, 0.0) - jnp.log1p(jnp.exp(-jnp.abs(f)))
    stack[4:5, :] = flags[...].astype(jnp.float32)
    run = stack[0:8, :]
    lane = lax.broadcasted_iota(jnp.int32, run.shape, 1)
    hop = 1
    while hop < length:
        run = run + jnp.where(lane >= hop, pltpu.roll(run, hop, 1), 0.0)
        hop *= 2
    stack[0:8, :] = run
    stack[8:8 + heads, :] = gates[0, 0:heads, :]
    cols[...] = stack[...].T

    def row(at):
        return stack[at:at + 1, :]

    def col(at):
        return cols[:, at:at + 1]

    def last(at):
        return stack[at:at + 1, length - 1:length]

    def own_state(h):
        end_row = jnp.where(row(4) == last(4), last(h) - row(h) + row(8 + h), very_low)
        top = jnp.max(end_row, axis=1, keepdims=True)
        end_col = jnp.where(col(4) == last(4), last(h) - col(h) + col(8 + h), very_low)
        weighted = (
            kv[:, h * dk:(h + 1) * dk].astype(jnp.float32) * jnp.exp(end_col - top)
        ).astype(jnp.bfloat16)
        own_mem[h] = dot(weighted, vv[:, h * dv:(h + 1) * dv], ((0,), (0,)))
        own_info[h:h + 1, :] = jnp.sum(weighted.astype(jnp.float32), axis=0, keepdims=True)
        own_info[heads + h:heads + h + 1, :] = jnp.broadcast_to(top, (1, dk))

    def decay(h):
        row_at = lax.broadcasted_iota(jnp.int32, (length, length), 0)
        col_at = lax.broadcasted_iota(jnp.int32, (length, length), 1)
        linked = jnp.logical_and(col(4) == row(4), row_at >= col_at)
        exponent = jnp.where(linked, col(h) - row(h) + row(8 + h), very_low)
        top = jnp.max(exponent, axis=1, keepdims=True)
        imax_scr[:, h:h + 1] = top
        prob[h] = jnp.exp(exponent - top) * factor

    def info_copy():
        return pltpu.make_async_remote_copy(
            src_ref=info_out, dst_ref=info_in, send_sem=ssend.at[heads], recv_sem=srecv.at[heads],
            device_id=up, device_id_type=MESH,
        )

    def mem_copy(h):
        return pltpu.make_async_remote_copy(
            src_ref=mem_out.at[h], dst_ref=mem_in.at[h], send_sem=ssend.at[h], recv_sem=srecv.at[h],
            device_id=up, device_id_type=MESH,
        )

    def pass_head(h):
        if h == 0:
            @pl.when(z > 0)
            def _():
                info_copy().wait_recv()

        @pl.when(z > 0)
        def _():
            mem_copy(h).wait_recv()

        @pl.when(z < Z - 1)
        def _():
            def blend(at):
                gap = jnp.where(last(4) > 0, very_low, last(at))
                shifted = info_in[heads + at:heads + at + 1, :] + gap
                top = own_info[heads + at:heads + at + 1, :]
                both = jnp.maximum(shifted, top)
                return both, jnp.exp(shifted - both), jnp.exp(top - both)

            if h == 0:
                for at in range(heads):
                    both, early, late = blend(at)
                    info_out[at:at + 1, :] = early * info_in[at:at + 1, :] + late * own_info[at:at + 1, :]
                    info_out[heads + at:heads + at + 1, :] = both
                info_copy().start()
            _, early, late = blend(h)
            mem_out[h] = (
                early[:, 0:1] * mem_in[h].astype(jnp.float32) + late[:, 0:1] * own_mem[h]
            ).astype(jnp.bfloat16)
            mem_copy(h).start()

    def start_state():
        for one in local[3:5]:
            one.wait()
        for h in range(heads):
            own_state(h)
        hand_on_first()

    def hand_on_first():
        @pl.when(z == 0)
        def _():
            mem_in[...] = jnp.zeros_like(mem_in)
            info_in[0:heads, :] = jnp.zeros((heads, dk), jnp.float32)
            info_in[heads:, :] = jnp.full((heads, dk), very_low, jnp.float32)
            for h in range(heads):
                pass_head(h)

    if not spread:
        start_state()

        @pl.when(z > 0)
        def _():
            for h in range(heads):
                pass_head(h)

        for h in range(heads):
            decay(h)
        for one in local[5:]:
            one.wait()

    def multiply(at, piece):
        part = xv[:, pl.ds(pl.multiple_of(at * rows, 128), rows)]
        acc[...] += dot(part, piece)

    if spread:
        state_steps = [pieces + heads + h for h in range(heads)]
        def places(s, low):
            q = (s + 2 * pieces) // pieces - 2
            p = (s + 2 * pieces) % pieces
            below, above = z - q, z + q
            yield below, p, jnp.logical_and(q >= low, jnp.logical_and(q < Z, below >= 0))
            yield above, p, jnp.logical_and(q >= max(low, 1), above < Z)

        def take(xx, cc, zz, p):
            @pl.when(p == pieces - 1)
            def _():
                multiply(shard(xx, cc, zz), wbuf[shard(xx, cc, zz)])

        def one_step(t, carry):
            for way, (zz, p, ok) in enumerate(places(t, 1)):
                @pl.when(ok)
                def _():
                    z_copy(way, zz, p).wait_recv()

                    @pl.when(z < Z - 1 if way == 0 else z > 0)
                    def _():
                        z_copy(way, zz, p).start()

                    x_copy(x, zz, p).start()
                    y_copy(x, zz, p, 1).start()
                    c_copy(x, c, zz, p, 0).start()

            for zz, p, ok in places(t - lag_across, 0):
                @pl.when(ok)
                def _():
                    x_copy(1 - x, zz, p).wait_recv()
                    @pl.when(jnp.logical_or(zz != z, p < pieces - early))
                    def _():
                        y_copy(1 - x, zz, p, 1).start()

                    c_copy(1 - x, c, zz, p, 0).start()

            for h in range(heads):
                @pl.when(t == pieces + h)
                def _():
                    if h == 0:
                        for one in local[3:5]:
                            one.wait()
                    own_state(h)

            @pl.when(t == pieces + heads)
            def _():
                hand_on_first()

            for h in range(heads):
                @pl.when(jnp.logical_and(t == z * 2 + state_steps[h], jnp.logical_and(z > 0, z < Z - 1)))
                def _():
                    pass_head(h)

            @pl.when(t == pieces + 1)
            def _():
                for one in local[5:]:
                    one.wait()
                acc[...] = dot(
                    xv[:, pl.ds(pl.multiple_of(shard(x, c, z) * rows, 128), rows)], wown[...]
                )

            for h in range(heads):
                @pl.when(t == 2 * pieces + h * (pieces // 2))
                def _():
                    decay(h)

            for zz, p, ok in places(t - lag_over, 1):
                @pl.when(ok)
                def _():
                    y_copy(x, zz, p, 2).wait_recv()
                    c_copy(x, c, zz, p, 2).start()
                    take(x, c, zz, p)

            for zz, p, ok in places(t - lag_over_across, 0):
                @pl.when(ok)
                def _():
                    whole = jnp.logical_and(zz == z, p >= pieces - early)

                    @pl.when(whole)
                    def _():
                        e_copy(1 - x, p).wait_recv()

                    @pl.when(jnp.logical_not(whole))
                    def _():
                        y_copy(1 - x, zz, p, 2).wait_recv()

                    c_copy(1 - x, c, zz, p, 2).start()
                    take(1 - x, c, zz, p)

            for zz, p, ok in places(t - lag_mate, 0):
                @pl.when(ok)
                def _():
                    for part in (0, 2):
                        c_copy(x, 1 - c, zz, p, part).wait_recv()
                    take(x, 1 - c, zz, p)

            for zz, p, ok in places(t - lag_mate_across, 0):
                @pl.when(ok)
                def _():
                    for part in (0, 2):
                        c_copy(1 - x, 1 - c, zz, p, part).wait_recv()
                    take(1 - x, 1 - c, zz, p)

            return carry

        lax.fori_loop(1, Z * pieces + lag_mate_across, one_step, 0)

        @pl.when(z == Z - 1)
        def _():
            for h in range(heads):
                pass_head(h)

    else:
        acc[...] = jnp.zeros_like(acc)

        def one_block(at, carry):
            multiply(at, wown[pl.ds(pl.multiple_of(at * rows, 16), rows), :])
            return carry

        lax.fori_loop(0, features // rows, one_block, 0)

    info = info_in[...]
    for h in range(heads):
        q = acc[:, h * dk:(h + 1) * dk].astype(jnp.bfloat16)
        values = vv[:, h * dv:(h + 1) * dv]
        scores = dot(q, kv[:, h * dk:(h + 1) * dk], ((1,), (1,)))
        weighted = (scores * prob[h]).astype(jnp.bfloat16)
        inner = dot(weighted, values)
        inner_den = jnp.sum(weighted.astype(jnp.float32), axis=1, keepdims=True)
        cross = dot(q, mem_in[h])
        normer = info[h:h + 1, :].astype(jnp.bfloat16).astype(jnp.float32)
        cross_den = jnp.sum(q.astype(jnp.float32) * normer, axis=1, keepdims=True)
        top = imax_scr[:, h:h + 1]
        carried = jnp.where(col(4) == 0, col(h) + info[heads + h:heads + h + 1, 0:1], very_low)
        row_max = jnp.maximum(top, carried)
        a = jnp.exp(top - row_max)
        b = jnp.exp(carried - row_max) * factor
        den = a * inner_den + b * cross_den
        inverse = 1.0 / jnp.maximum(jnp.abs(den), jnp.exp(jnp.maximum(-row_max, 0.0)))
        hidden = (a * inverse) * inner + (b * inverse) * cross
        out_ref[0, :, h * dv:(h + 1) * dv] = hidden.astype(jnp.bfloat16)

    @pl.when(z < Z - 1)
    def _():
        info_copy().wait_send()
        for h in range(heads):
            mem_copy(h).wait_send()

    if spread:
        def drain(sem, count, tall, wide):
            some = wbuf.at[0:count, 0:tall, 0:wide]
            pltpu.make_async_remote_copy(
                src_ref=some, dst_ref=some, send_sem=sem, recv_sem=sem, device_id=mate, device_id_type=MESH
            ).wait_send()

        for at in range(Z):
            @pl.when(z == at)
            def _():
                if at < Z - 1:
                    drain(zsend.at[0], at + 1, rows, A + B)
                if at > 0:
                    drain(zsend.at[1], Z - at, rows, A + B)

        drain(xsend.at[0], Z, rows, A + B)
        drain(esend.at[0], 1, early * high, A)
        drain(ysend.at[x], Z - 1, rows, A)
        drain(ysend.at[1 - x], Z * pieces - early, high, A)
        drain(csend.at[0], 2 * Z, rows, width)


def body(Z, dp, planes, normed_input, query_weight, key_vectors, value_vectors, input_gate, forget_gate, resets):
    _, length, features = normed_input.shape
    heads = input_gate.shape[1]
    width = query_weight.shape[1]
    dk = key_vectors.shape[2] // heads
    dv = value_vectors.shape[2] // heads
    spread = dp == 4 and planes == 2 and query_weight.shape[0] % 256 == 0
    if spread:
        rows = query_weight.shape[0]
        weight = query_weight
    else:
        rows = 256
        weight = lax.all_gather(query_weight, ("dp", "ctx"), axis=0, tiled=True)
    count = features // rows if spread else 1
    dma = pltpu.SemaphoreType.DMA
    hbm = pl.BlockSpec(memory_space=pltpu.HBM)
    vmem = pl.BlockSpec(memory_space=pltpu.VMEM)
    return pl.pallas_call(
        functools.partial(kernel, spread, Z, heads),
        out_shape=jax.ShapeDtypeStruct((1, length, heads * dv), jnp.bfloat16),
        in_specs=[hbm] * 7,
        out_specs=vmem,
        scratch_shapes=[
            pltpu.VMEM((2, 8, length), jnp.float32),
            pltpu.VMEM((1, length), jnp.int32),
            pltpu.VMEM((length, features), jnp.bfloat16),
            pltpu.VMEM((length, heads * dk), jnp.bfloat16),
            pltpu.VMEM((length, heads * dv), jnp.bfloat16),
            pltpu.VMEM(weight.shape, jnp.bfloat16),
            pltpu.VMEM((count, rows, width), jnp.bfloat16),
            pltpu.VMEM((length, width), jnp.float32),
            pltpu.VMEM((heads, length, length), jnp.float32),
            pltpu.VMEM((128, length), jnp.float32),
            pltpu.VMEM((length, 128), jnp.float32),
            pltpu.VMEM((length, 128), jnp.float32),
            pltpu.VMEM((heads, dk, dv), jnp.float32),
            pltpu.VMEM((2 * heads, dk), jnp.float32),
            pltpu.VMEM((heads, dk, dv), jnp.bfloat16),
            pltpu.VMEM((2 * heads, dk), jnp.float32),
            pltpu.VMEM((heads, dk, dv), jnp.bfloat16),
            pltpu.VMEM((2 * heads, dk), jnp.float32),
            dma((7,)),
            dma((2,)), dma((Z, pieces)),
            dma((1,)), dma((Z, pieces)),
            dma((1,)), dma((pieces,)),
            dma((2,)), dma((2, Z, pieces)),
            dma((1,)), dma((2, Z, pieces, 2)),
            dma((heads + 1,)), dma((heads + 1,)),
        ],
        compiler_params=pltpu.CompilerParams(
            collective_id=0, has_side_effects=True, vmem_limit_bytes=60 * 1024 * 1024
        ),
        cost_estimate=pl.CostEstimate(
            flops=2 * length * features * width, bytes_accessed=6 * 1024 * 1024, transcendentals=0
        ),
    )(normed_input, weight, key_vectors, value_vectors, input_gate, forget_gate, resets)


def solution(mesh):
    sizes = mesh.shape
    return jax.shard_map(
        functools.partial(body, sizes["ctx"], sizes["dp"], sizes["groups"]),
        mesh=mesh,
        in_specs=(
            P(("groups", "dp"), "ctx", None),
            P(("dp", "ctx"), None),
            P(("groups", "dp"), "ctx", None),
            P(("groups", "dp"), "ctx", None),
            P(("groups", "dp"), None, "ctx"),
            P(("groups", "dp"), None, "ctx"),
            P(("groups", "dp"), "ctx"),
        ),
        out_specs=P(("groups", "dp"), "ctx", None),
        check_vma=False,
    )
```

```python
import functools

import jax
import jax.numpy as jnp
from jax import lax
from jax.experimental import pallas as pl
from jax.experimental.pallas import tpu as pltpu
from jax.sharding import PartitionSpec as P

very_low = -1e30
shared_columns = 384
pieces = 4
early = 2
lag_across, lag_over, lag_over_across, lag_mate, lag_mate_across = 2, 2, 4, 5, 7
MESH = pl.DeviceIdType.MESH


def dot(a, b, dims=((1,), (0,))):
    return lax.dot_general(a, b, (dims, ((), ())), preferred_element_type=jnp.float32)


def kernel(
    spread, Z, heads, x_hbm, w_hbm, k_hbm, v_hbm, ig_hbm, fg_hbm, rs_hbm, out_ref,
    gates, flags, xv, kv, vv, wown, wbuf, acc, prob, stack, cols, imax_scr, own_mem, own_info,
    mem_in, info_in, mem_out, info_out,
    lsem, zsend, zrecv, xsend, xrecv, esend, erecv, ysend, yrecv, csend, crecv, ssend, srecv,
):
    y = lax.axis_index("groups")
    d = lax.axis_index("dp")
    z = lax.axis_index("ctx")
    x, c = d // 2, d % 2
    up, down = (y, d, z + 1), (y, d, z - 1)
    across = (y, (1 - x) * 2 + c, z)
    over = (1 - y, d, z)
    mate = (y, x * 2 + 1 - c, z)
    length, features = xv.shape
    dk = kv.shape[1] // heads
    dv = vv.shape[1] // heads
    factor = dk ** (-0.5)
    width = acc.shape[1]
    rows = wbuf.shape[1]
    A = shared_columns

    local = [
        pltpu.make_async_copy(ig_hbm.at[0], gates.at[0, 0:heads], lsem.at[4]),
        pltpu.make_async_copy(fg_hbm.at[0], gates.at[1, 0:heads], lsem.at[5]),
        pltpu.make_async_copy(rs_hbm, flags, lsem.at[6]),
        pltpu.make_async_copy(k_hbm.at[0], kv, lsem.at[0]),
        pltpu.make_async_copy(v_hbm.at[0], vv, lsem.at[1]),
        pltpu.make_async_copy(x_hbm.at[0], xv, lsem.at[2]),
        pltpu.make_async_copy(w_hbm, wown, lsem.at[3]),
    ]
    for one in local:
        one.start()

    barrier = pltpu.get_barrier_semaphore()

    def greet(device):
        pl.semaphore_signal(barrier, inc=1, device_id=device, device_id_type=MESH)

    @pl.when(z < Z - 1)
    def _():
        greet(up)

    @pl.when(z > 0)
    def _():
        greet(down)

    base = 0
    if spread:
        for device in (across, over, mate):
            greet(device)
        base = 3
    pl.semaphore_wait(
        barrier, base + jnp.where(z > 0, 1, 0) + jnp.where(z < Z - 1, 1, 0)
    )

    B = width - 2 * A

    def columns(part):
        if part == 0:
            return pl.ds(pl.multiple_of(y * A, 128), A + B)
        if part == 1:
            return pl.ds(pl.multiple_of(y * (A + B), 128), A)
        return pl.ds(pl.multiple_of((1 - y) * (A + B), 128), A)

    high = rows // pieces

    def shard(xx, cc, zz):
        return (xx * 2 + cc) * Z + zz

    def remote(xx, cc, zz, p, part, send, recv, device, own=False):
        at = pl.ds(p * high if isinstance(p, int) else pl.multiple_of(p * high, 16), high)
        there = wbuf.at[shard(xx, cc, zz), at, columns(part)]
        here = w_hbm.at[at, columns(part)] if own else there
        return pltpu.make_async_remote_copy(
            src_ref=here, dst_ref=there, send_sem=send, recv_sem=recv,
            device_id=device, device_id_type=MESH,
        )

    def z_copy(way, zz, p, own=False):
        device = up if way == 0 else down
        return remote(x, c, zz, p, 0, zsend.at[way], zrecv.at[zz, p], device, own)

    def x_copy(xx, zz, p, own=False):
        return remote(xx, c, zz, p, 0, xsend.at[0], xrecv.at[zz, p], across, own)

    def e_copy(xx, p, own=False):
        return remote(xx, c, z, p, 2, esend.at[0], erecv.at[p], across, own)

    def y_copy(xx, zz, p, part):
        return remote(xx, c, zz, p, part, ysend.at[xx], yrecv.at[xx, zz, p], over)

    def c_copy(xx, cc, zz, p, part, own=False):
        return remote(
            xx, cc, zz, p, part, csend.at[0], crecv.at[xx, zz, p, part // 2], mate, own
        )

    if spread:
        for p in range(pieces):
            @pl.when(z < Z - 1)
            def _():
                z_copy(0, z, p, True).start()

            @pl.when(z > 0)
            def _():
                z_copy(1, z, p, True).start()

            x_copy(x, z, p, True).start()
            if p >= pieces - early:
                e_copy(x, p, True).start()
        for p in range(pieces):
            for part in (0, 2):
                c_copy(x, c, z, p, part, True).start()

    for one in local[:3]:
        one.wait()

    f = gates[1, 0:heads, :]
    stack[...] = jnp.zeros_like(stack)
    stack[0:heads, :] = jnp.minimum(f, 0.0) - jnp.log1p(jnp.exp(-jnp.abs(f)))
    stack[4:5, :] = flags[...].astype(jnp.float32)
    run = stack[0:8, :]
    lane = lax.broadcasted_iota(jnp.int32, run.shape, 1)
    hop = 1
    while hop < length:
        run = run + jnp.where(lane >= hop, pltpu.roll(run, hop, 1), 0.0)
        hop *= 2
    stack[0:8, :] = run
    stack[8:8 + heads, :] = gates[0, 0:heads, :]
    cols[...] = stack[...].T

    def row(at):
        return stack[at:at + 1, :]

    def col(at):
        return cols[:, at:at + 1]

    def last(at):
        return stack[at:at + 1, length - 1:length]

    def own_state(h):
        end_row = jnp.where(row(4) == last(4), last(h) - row(h) + row(8 + h), very_low)
        top = jnp.max(end_row, axis=1, keepdims=True)
        end_col = jnp.where(col(4) == last(4), last(h) - col(h) + col(8 + h), very_low)
        weighted = (
            kv[:, h * dk:(h + 1) * dk].astype(jnp.float32) * jnp.exp(end_col - top)
        ).astype(jnp.bfloat16)
        own_mem[h] = dot(weighted, vv[:, h * dv:(h + 1) * dv], ((0,), (0,)))
        own_info[h:h + 1, :] = jnp.sum(weighted.astype(jnp.float32), axis=0, keepdims=True)
        own_info[heads + h:heads + h + 1, :] = jnp.broadcast_to(top, (1, dk))

    def decay(h):
        row_at = lax.broadcasted_iota(jnp.int32, (length, length), 0)
        col_at = lax.broadcasted_iota(jnp.int32, (length, length), 1)
        linked = jnp.logical_and(col(4) == row(4), row_at >= col_at)
        exponent = jnp.where(linked, col(h) - row(h) + row(8 + h), very_low)
        top = jnp.max(exponent, axis=1, keepdims=True)
        imax_scr[:, h:h + 1] = top
        prob[h] = jnp.exp(exponent - top) * factor

    def info_copy():
        return pltpu.make_async_remote_copy(
            src_ref=info_out, dst_ref=info_in, send_sem=ssend.at[heads], recv_sem=srecv.at[heads],
            device_id=up, device_id_type=MESH,
        )

    def mem_copy(h):
        return pltpu.make_async_remote_copy(
            src_ref=mem_out.at[h], dst_ref=mem_in.at[h], send_sem=ssend.at[h], recv_sem=srecv.at[h],
            device_id=up, device_id_type=MESH,
        )

    def pass_head(h):
        if h == 0:
            @pl.when(z > 0)
            def _():
                info_copy().wait_recv()

        @pl.when(z > 0)
        def _():
            mem_copy(h).wait_recv()

        @pl.when(z < Z - 1)
        def _():
            def blend(at):
                gap = jnp.where(last(4) > 0, very_low, last(at))
                shifted = info_in[heads + at:heads + at + 1, :] + gap
                top = own_info[heads + at:heads + at + 1, :]
                both = jnp.maximum(shifted, top)
                return both, jnp.exp(shifted - both), jnp.exp(top - both)

            if h == 0:
                for at in range(heads):
                    both, early, late = blend(at)
                    info_out[at:at + 1, :] = early * info_in[at:at + 1, :] + late * own_info[at:at + 1, :]
                    info_out[heads + at:heads + at + 1, :] = both
                info_copy().start()
            _, early, late = blend(h)
            mem_out[h] = (
                early[:, 0:1] * mem_in[h].astype(jnp.float32) + late[:, 0:1] * own_mem[h]
            ).astype(jnp.bfloat16)
            mem_copy(h).start()

    def start_state():
        for one in local[3:5]:
            one.wait()
        for h in range(heads):
            own_state(h)

        @pl.when(z == 0)
        def _():
            mem_in[...] = jnp.zeros_like(mem_in)
            info_in[0:heads, :] = jnp.zeros((heads, dk), jnp.float32)
            info_in[heads:, :] = jnp.full((heads, dk), very_low, jnp.float32)
            for h in range(heads):
                pass_head(h)

    if not spread:
        start_state()

        @pl.when(z > 0)
        def _():
            for h in range(heads):
                pass_head(h)

        for h in range(heads):
            decay(h)
        for one in local[5:]:
            one.wait()

    def multiply(at, piece):
        part = xv[:, pl.ds(pl.multiple_of(at * rows, 128), rows)]
        acc[...] += dot(part, piece)

    if spread:
        state_steps = [-(-2 * pieces * (h + 1) // 5) for h in range(heads)]
        def places(s, low):
            q = (s + 2 * pieces) // pieces - 2
            p = (s + 2 * pieces) % pieces
            below, above = z - q, z + q
            yield below, p, jnp.logical_and(q >= low, jnp.logical_and(q < Z, below >= 0))
            yield above, p, jnp.logical_and(q >= max(low, 1), above < Z)

        def take(xx, cc, zz, p):
            @pl.when(p == pieces - 1)
            def _():
                multiply(shard(xx, cc, zz), wbuf[shard(xx, cc, zz)])

        def one_step(t, carry):
            for way, (zz, p, ok) in enumerate(places(t, 1)):
                @pl.when(ok)
                def _():
                    z_copy(way, zz, p).wait_recv()

                    @pl.when(z < Z - 1 if way == 0 else z > 0)
                    def _():
                        z_copy(way, zz, p).start()

                    x_copy(x, zz, p).start()
                    y_copy(x, zz, p, 1).start()
                    c_copy(x, c, zz, p, 0).start()

            for zz, p, ok in places(t - lag_across, 0):
                @pl.when(ok)
                def _():
                    x_copy(1 - x, zz, p).wait_recv()
                    @pl.when(jnp.logical_or(zz != z, p < pieces - early))
                    def _():
                        y_copy(1 - x, zz, p, 1).start()

                    c_copy(1 - x, c, zz, p, 0).start()

            for h in range(heads):
                @pl.when(jnp.logical_and(t == z * pieces + state_steps[h], jnp.logical_and(z > 0, z < Z - 1)))
                def _():
                    pass_head(h)

            @pl.when(t == lag_across + 1)
            def _():
                start_state()
                for one in local[5:]:
                    one.wait()
                acc[...] = dot(
                    xv[:, pl.ds(pl.multiple_of(shard(x, c, z) * rows, 128), rows)], wown[...]
                )

            for h in range(heads):
                @pl.when(t == pieces + 1 + h * (pieces // 2))
                def _():
                    decay(h)

            for zz, p, ok in places(t - lag_over, 1):
                @pl.when(ok)
                def _():
                    y_copy(x, zz, p, 2).wait_recv()
                    c_copy(x, c, zz, p, 2).start()
                    take(x, c, zz, p)

            for zz, p, ok in places(t - lag_over_across, 0):
                @pl.when(ok)
                def _():
                    whole = jnp.logical_and(zz == z, p >= pieces - early)

                    @pl.when(whole)
                    def _():
                        e_copy(1 - x, p).wait_recv()

                    @pl.when(jnp.logical_not(whole))
                    def _():
                        y_copy(1 - x, zz, p, 2).wait_recv()

                    c_copy(1 - x, c, zz, p, 2).start()
                    take(1 - x, c, zz, p)

            for zz, p, ok in places(t - lag_mate, 0):
                @pl.when(ok)
                def _():
                    for part in (0, 2):
                        c_copy(x, 1 - c, zz, p, part).wait_recv()
                    take(x, 1 - c, zz, p)

            for zz, p, ok in places(t - lag_mate_across, 0):
                @pl.when(ok)
                def _():
                    for part in (0, 2):
                        c_copy(1 - x, 1 - c, zz, p, part).wait_recv()
                    take(1 - x, 1 - c, zz, p)

            return carry

        lax.fori_loop(1, Z * pieces + lag_mate_across, one_step, 0)

        @pl.when(z == Z - 1)
        def _():
            for h in range(heads):
                pass_head(h)

    else:
        acc[...] = jnp.zeros_like(acc)

        def one_block(at, carry):
            multiply(at, wown[pl.ds(pl.multiple_of(at * rows, 16), rows), :])
            return carry

        lax.fori_loop(0, features // rows, one_block, 0)

    info = info_in[...]
    for h in range(heads):
        q = acc[:, h * dk:(h + 1) * dk].astype(jnp.bfloat16)
        values = vv[:, h * dv:(h + 1) * dv]
        scores = dot(q, kv[:, h * dk:(h + 1) * dk], ((1,), (1,)))
        weighted = (scores * prob[h]).astype(jnp.bfloat16)
        inner = dot(weighted, values)
        inner_den = jnp.sum(weighted.astype(jnp.float32), axis=1, keepdims=True)
        cross = dot(q, mem_in[h])
        normer = info[h:h + 1, :].astype(jnp.bfloat16).astype(jnp.float32)
        cross_den = jnp.sum(q.astype(jnp.float32) * normer, axis=1, keepdims=True)
        top = imax_scr[:, h:h + 1]
        carried = jnp.where(col(4) == 0, col(h) + info[heads + h:heads + h + 1, 0:1], very_low)
        row_max = jnp.maximum(top, carried)
        a = jnp.exp(top - row_max)
        b = jnp.exp(carried - row_max) * factor
        den = a * inner_den + b * cross_den
        inverse = 1.0 / jnp.maximum(jnp.abs(den), jnp.exp(jnp.maximum(-row_max, 0.0)))
        hidden = (a * inverse) * inner + (b * inverse) * cross
        out_ref[0, :, h * dv:(h + 1) * dv] = hidden.astype(jnp.bfloat16)

    @pl.when(z < Z - 1)
    def _():
        info_copy().wait_send()
        for h in range(heads):
            mem_copy(h).wait_send()

    if spread:
        def drain(sem, count, tall, wide):
            some = wbuf.at[0:count, 0:tall, 0:wide]
            pltpu.make_async_remote_copy(
                src_ref=some, dst_ref=some, send_sem=sem, recv_sem=sem, device_id=mate, device_id_type=MESH
            ).wait_send()

        for at in range(Z):
            @pl.when(z == at)
            def _():
                if at < Z - 1:
                    drain(zsend.at[0], at + 1, rows, A + B)
                if at > 0:
                    drain(zsend.at[1], Z - at, rows, A + B)

        drain(xsend.at[0], Z, rows, A + B)
        drain(esend.at[0], 1, early * high, A)
        drain(ysend.at[x], Z - 1, rows, A)
        drain(ysend.at[1 - x], Z * pieces - early, high, A)
        drain(csend.at[0], 2 * Z, rows, width)


def body(Z, dp, planes, normed_input, query_weight, key_vectors, value_vectors, input_gate, forget_gate, resets):
    _, length, features = normed_input.shape
    heads = input_gate.shape[1]
    width = query_weight.shape[1]
    dk = key_vectors.shape[2] // heads
    dv = value_vectors.shape[2] // heads
    spread = dp == 4 and planes == 2 and query_weight.shape[0] % 256 == 0
    if spread:
        rows = query_weight.shape[0]
        weight = query_weight
    else:
        rows = 256
        weight = lax.all_gather(query_weight, ("dp", "ctx"), axis=0, tiled=True)
    count = features // rows if spread else 1
    dma = pltpu.SemaphoreType.DMA
    hbm = pl.BlockSpec(memory_space=pltpu.HBM)
    vmem = pl.BlockSpec(memory_space=pltpu.VMEM)
    return pl.pallas_call(
        functools.partial(kernel, spread, Z, heads),
        out_shape=jax.ShapeDtypeStruct((1, length, heads * dv), jnp.bfloat16),
        in_specs=[hbm] * 7,
        out_specs=vmem,
        scratch_shapes=[
            pltpu.VMEM((2, 8, length), jnp.float32),
            pltpu.VMEM((1, length), jnp.int32),
            pltpu.VMEM((length, features), jnp.bfloat16),
            pltpu.VMEM((length, heads * dk), jnp.bfloat16),
            pltpu.VMEM((length, heads * dv), jnp.bfloat16),
            pltpu.VMEM(weight.shape, jnp.bfloat16),
            pltpu.VMEM((count, rows, width), jnp.bfloat16),
            pltpu.VMEM((length, width), jnp.float32),
            pltpu.VMEM((heads, length, length), jnp.float32),
            pltpu.VMEM((128, length), jnp.float32),
            pltpu.VMEM((length, 128), jnp.float32),
            pltpu.VMEM((length, 128), jnp.float32),
            pltpu.VMEM((heads, dk, dv), jnp.float32),
            pltpu.VMEM((2 * heads, dk), jnp.float32),
            pltpu.VMEM((heads, dk, dv), jnp.bfloat16),
            pltpu.VMEM((2 * heads, dk), jnp.float32),
            pltpu.VMEM((heads, dk, dv), jnp.bfloat16),
            pltpu.VMEM((2 * heads, dk), jnp.float32),
            dma((7,)),
            dma((2,)), dma((Z, pieces)),
            dma((1,)), dma((Z, pieces)),
            dma((1,)), dma((pieces,)),
            dma((2,)), dma((2, Z, pieces)),
            dma((1,)), dma((2, Z, pieces, 2)),
            dma((heads + 1,)), dma((heads + 1,)),
        ],
        compiler_params=pltpu.CompilerParams(
            collective_id=0, has_side_effects=True, vmem_limit_bytes=60 * 1024 * 1024
        ),
        cost_estimate=pl.CostEstimate(
            flops=2 * length * features * width, bytes_accessed=6 * 1024 * 1024, transcendentals=0
        ),
    )(normed_input, weight, key_vectors, value_vectors, input_gate, forget_gate, resets)


def solution(mesh):
    sizes = mesh.shape
    return jax.shard_map(
        functools.partial(body, sizes["ctx"], sizes["dp"], sizes["groups"]),
        mesh=mesh,
        in_specs=(
            P(("groups", "dp"), "ctx", None),
            P(("dp", "ctx"), None),
            P(("groups", "dp"), "ctx", None),
            P(("groups", "dp"), "ctx", None),
            P(("groups", "dp"), None, "ctx"),
            P(("groups", "dp"), None, "ctx"),
            P(("groups", "dp"), "ctx"),
        ),
        out_specs=P(("groups", "dp"), "ctx", None),
        check_vma=False,
    )
```
